256 devices in a mesh: cell: 32 (over x_hi, z, core), chrom: 8 (over x_lo, y).
Axes of the slice: x: 4 (x_hi: 2, x_lo: 2; x = x_hi * 2 + x_lo), y: 4, z: 8, core: 2. Of those that a mesh axis runs over, the one named last changes fastest.
Arguments:
- cell_factors: bfloat16 [32768, 256], P('cell'), may hold values from -6 to 6
- peak_factors: bfloat16 [524288, 256], P(('cell', 'chrom')), may hold values from -6 to 6
- tile_values: bfloat16 [96, 256, 128, 128], P('cell', 'chrom'), may hold values from -6 to 6
- tile_index: int32 [96, 256], P('cell', 'chrom'), may hold values from 0 to 127, as said below
- tile_counts: int32 [96, 8], P('cell', 'chrom'), may hold values from 8 to 32, as said below
Outputs:
- peak_out: bfloat16 [524288, 256], P(('cell', 'chrom'))
- cell_grads: float32 [32768, 256], P(('cell', 'chrom'))
The draws below stay inside these ranges and needn't reach their ends.
Inputs may be any that keep to these rules, and one draw needn't show every extreme that they name: `tile_index`: within one cell index, stratum and chrom group the 32 numbers are distinct. `tile_counts`: in every stratum one cell index has 32 live slots in every chrom group; every other count is 32, 16 or 8.
All inputs are finite; a program needn't handle non-finite values.
Results may differ from the reference program's by a relative error of at most 0.015.
Values may be sent and summed in bfloat16 or wider, within the bound.
No kernel may reach another device: no remote copies, remote signals or barrier semaphores. Data moves between devices by JAX's collectives and lax.ppermute only.
A program may use at most 64 MiB of HBM per device.

```python
import math
import jax
import jax.numpy as jnp
from jax import lax

K = 256
TILE = 128
STRATA = 3
ROWT = 8
COLT = 16
TMAX = 32
GROUP_BLOCKS = 32
CHROMS = 8
CELLS = 32768
PEAKS = 524288
N_CELL = 32
N_CHROM = 8


def draw_tile_index(key, part):
    key = jax.random.fold_in(key, 11)
    grid_size = ROWT * COLT
    scores = jax.random.randint(key, (N_CELL * STRATA, N_CHROM, grid_size), 0, 65536)
    scores = scores * grid_size + jnp.arange(grid_size, dtype=jnp.int32)
    ordering = jnp.argsort(scores, axis=-1)[..., :TMAX]
    return ordering.astype(jnp.int32).reshape(N_CELL * STRATA, N_CHROM * TMAX)


def draw_tile_counts(key, part):
    key = jax.random.fold_in(key, 12)
    first_key, second_key = jax.random.split(key)
    halving = jax.random.randint(first_key, (N_CELL, STRATA, N_CHROM), 0, 3)
    counts = jnp.where(halving == 0, TMAX, jnp.where(halving == 1, TMAX // 2, TMAX // 4))
    busiest = jax.random.randint(second_key, (STRATA,), 0, N_CELL)
    chosen = jnp.arange(N_CELL)[:, None] == busiest[None, :]
    counts = jnp.where(chosen[:, :, None], TMAX, counts)
    return counts.astype(jnp.int32).reshape(N_CELL * STRATA, N_CHROM)


def shard_levels(key, shape, shards, least, top_value):
    loudness, own = 1.0, jax.random.fold_in(key, 6)
    for dim, shards_of in shards:
        draws = jnp.exp(jax.random.uniform(jax.random.fold_in(own, dim), (shards_of,), jnp.float32, least / len(shards), top_value / len(shards)))
        loudness = loudness * jnp.repeat(draws, shape[dim] // shards_of).reshape([-1 if axis == dim else 1 for axis in range(len(shape))])
    return loudness


def gaussian(own_key, dims, scale, most, cuts=(), held_as=jnp.bfloat16):
    gain = shard_levels(own_key, dims, cuts, -0.22, 0.18) if cuts else 1.0
    result = jax.random.normal(own_key, dims, jnp.float32) * scale * gain
    return jnp.minimum(jnp.maximum(result, -most), most).astype(held_as)


def setup_inputs(seed: int = 0) -> dict:
    streams_of = jax.random.split(jax.random.key(seed), 6)
    return {
        "cell_factors": gaussian(streams_of[0], (CELLS, K), 1.0, 6.0, ((0, 32),)),
        "peak_factors": gaussian(streams_of[1], (PEAKS, K), 1.0, 6.0, ((0, 256),)),
        "tile_values": gaussian(streams_of[2], (STRATA * N_CELL, TMAX * N_CHROM, TILE, TILE), 1.0, 6.0, ((0, 32), (1, 8))),
        "tile_index": draw_tile_index(jax.random.fold_in(streams_of[5], 71), 0),
        "tile_counts": draw_tile_counts(jax.random.fold_in(streams_of[5], 71), 0),
    }


learning_rate = 0.15
gradient_scale = 0.1

def update_block(cell_block, peak_block, values, index, live_count):
    peak_cols = index % COLT
    cell_rows = index // COLT
    left_tiles = cell_block[cell_rows].astype(jnp.float32)
    right_tiles = peak_block[peak_cols].astype(jnp.float32)
    scaling = 1.0 / math.sqrt(K)
    predicted = jnp.einsum('tak,tbk->tab', left_tiles, right_tiles) * scaling
    live_mask = jnp.arange(TMAX, dtype=jnp.int32) < live_count
    residual = jnp.where(live_mask[:, None, None], predicted - values.astype(jnp.float32), 0.0).astype(jnp.bfloat16)
    residual = lax.optimization_barrier(residual)
    resid_wide = residual.astype(jnp.float32)
    peak_terms = jnp.einsum('tab,tak->tbk', resid_wide, left_tiles) * scaling
    cell_terms = jnp.einsum('tab,tbk->tak', resid_wide, right_tiles) * scaling
    peak_grad = jnp.zeros((COLT, TILE, K), jnp.float32).at[peak_cols].add(peak_terms)
    cell_grad = jnp.zeros((ROWT, TILE, K), jnp.float32).at[cell_rows].add(cell_terms)
    new_block = (peak_block.astype(jnp.float32) - learning_rate * peak_grad).astype(jnp.bfloat16)
    return (lax.optimization_barrier(new_block), cell_grad)

def one_cell(pieces):
    cell_block, peak_row, values, index, counts = pieces
    return jax.vmap(update_block, in_axes=(None, 0, 0, 0, 0))(cell_block, peak_row, values, index, counts)

def reference(cell_factors, peak_factors, tile_values, tile_index, tile_counts):
    cell_blocks = cell_factors.reshape(GROUP_BLOCKS, ROWT, TILE, K)
    peaks = peak_factors.reshape(GROUP_BLOCKS, CHROMS, COLT, TILE, K)
    values = tile_values.reshape(GROUP_BLOCKS, STRATA, CHROMS, TMAX, TILE, TILE)
    index = tile_index.reshape(GROUP_BLOCKS, STRATA, CHROMS, TMAX)
    counts = tile_counts.reshape(GROUP_BLOCKS, STRATA, CHROMS)
    grads = jnp.zeros((GROUP_BLOCKS, ROWT, TILE, K), jnp.float32)
    for stratum in range(STRATA):
        held_now = jnp.roll(peaks, -stratum, axis=0)
        new_held, cell_part = lax.map(one_cell, (cell_blocks, held_now, values[:, stratum], index[:, stratum], counts[:, stratum]))
        grads = grads + lax.optimization_barrier(jnp.sum(cell_part, axis=1))
        peaks = jnp.roll(new_held, stratum, axis=0)
    cell_grads = (gradient_scale * grads).reshape(CELLS, K)
    return (peaks.reshape(PEAKS, K), cell_grads)
```

```python
import math

import jax
import jax.numpy as jnp
from jax import lax
from jax.experimental import pallas as pl
from jax.experimental.pallas import tpu as pltpu
from jax.sharding import PartitionSpec as P

learning_rate = 0.15
gradient_scale = 0.1


def passed_along(value, axis, by):
    count = lax.axis_size(axis)
    return lax.ppermute(value, axis, [(i, (i + by) % count) for i in range(count)])


def stratum_kernel(scaling, first, count_ref, index_ref, cell_ref, peak_ref, values_ref, *refs):
    if first:
        new_ref, grad_ref, peak_grad = refs
    else:
        old_ref, new_ref, grad_ref, peak_grad = refs
    peak_tiles = peak_ref.shape[0]
    peak_grad[...] = jnp.zeros_like(peak_grad)
    grad_ref[...] = jnp.zeros_like(grad_ref) if first else old_ref[...]
    unroll = 4

    def group(g, carry):
        for k in range(unroll):
            t = g * unroll + k
            place = index_ref[0, t]
            row = place // peak_tiles
            col = place % peak_tiles
            left = cell_ref[row]
            right = peak_ref[col]
            predicted = lax.dot_general(
                left, right, (((1,), (1,)), ((), ())), preferred_element_type=jnp.float32
            )
            resid = (predicted * scaling - values_ref[0, t].astype(jnp.float32)).astype(jnp.bfloat16)
            peak_grad[col] += lax.dot_general(
                resid, left, (((0,), (0,)), ((), ())), preferred_element_type=jnp.float32
            )
            grad_ref[row] += lax.dot_general(
                resid, right, (((1,), (0,)), ((), ())), preferred_element_type=jnp.float32
            )
        return carry

    lax.fori_loop(0, count_ref[0, 0] // unroll, group, 0)
    for c in range(peak_tiles):
        new_ref[c] = (
            peak_ref[c].astype(jnp.float32) - learning_rate * (peak_grad[c] * scaling)
        ).astype(new_ref.dtype)


def stratum_update(cell_blocks, peak_block, values, index, counts, grad, stratum):
    row_tiles, tile_size, rank_width = cell_blocks.shape
    slots = values.shape[1]
    scaling = 1.0 / math.sqrt(rank_width)
    first = grad is None
    smem = pl.BlockSpec(memory_space=pltpu.SMEM)
    vmem = pl.BlockSpec(memory_space=pltpu.VMEM)
    in_specs = [
        smem,
        smem,
        vmem,
        vmem,
        pl.BlockSpec((1,) + values.shape[1:], lambda i: (stratum, 0, 0, 0)),
    ]
    args = [counts[stratum : stratum + 1], index[stratum : stratum + 1], cell_blocks, peak_block, values]
    if not first:
        in_specs.append(vmem)
        args.append(grad)
    flops = 6 * slots * tile_size * tile_size * rank_width
    return pl.pallas_call(
        lambda *refs: stratum_kernel(scaling, first, *refs),
        grid=(1,),
        out_shape=(
            jax.ShapeDtypeStruct(peak_block.shape, peak_block.dtype),
            jax.ShapeDtypeStruct(cell_blocks.shape, jnp.float32),
        ),
        in_specs=in_specs,
        out_specs=(vmem, vmem),
        scratch_shapes=[pltpu.VMEM(peak_block.shape, jnp.float32)],
        compiler_params=pltpu.CompilerParams(vmem_limit_bytes=24 * 1024 * 1024),
        cost_estimate=pl.CostEstimate(flops=flops, bytes_accessed=4 << 20, transcendentals=0),
    )(*args)


def per_device(cell_factors, peak_factors, tile_values, tile_index, tile_counts):
    cell_dev, rank_width = cell_factors.shape
    tile_size = tile_values.shape[-1]
    strata = tile_values.shape[0]
    block_rows = peak_factors.shape[0]
    row_tiles = cell_dev // tile_size
    peak_tiles = block_rows // tile_size
    chroms = lax.axis_size("chrom")
    share_rows = cell_dev // chroms
    cell_blocks = cell_factors.reshape(row_tiles, tile_size, rank_width)
    peak_block = peak_factors.reshape(peak_tiles, tile_size, rank_width)
    grad = None
    for stratum in range(strata):
        if stratum > 0:
            peak_block = passed_along(peak_block, "cell", -1)
        peak_block, grad = stratum_update(
            cell_blocks, peak_block, tile_values, tile_index, tile_counts, grad, stratum
        )
    peak_block = passed_along(peak_block, "cell", strata - 1)
    scale = gradient_scale / math.sqrt(rank_width)
    local_sum = (grad.reshape(cell_dev, rank_width) * scale).astype(jnp.bfloat16)
    shares = lax.all_to_all(local_sum, "chrom", 0, 0, tiled=True)
    summed = jnp.sum(shares.reshape(chroms, share_rows, rank_width).astype(jnp.float32), axis=0)
    return (peak_block.reshape(block_rows, rank_width), summed)


def solution(mesh):
    in_specs = (
        P("cell", None),
        P(("cell", "chrom"), None),
        P("cell", "chrom", None, None),
        P("cell", "chrom"),
        P("cell", "chrom"),
    )
    out_specs = (P(("cell", "chrom"), None), P(("cell", "chrom"), None))
    return jax.shard_map(
        per_device, mesh=mesh, in_specs=in_specs, out_specs=out_specs, check_vma=False
    )
```

```python
import functools
import math

import jax
import jax.numpy as jnp
from jax import lax
from jax.experimental import pallas as pl
from jax.experimental.pallas import tpu as pltpu
from jax.sharding import PartitionSpec as P

learning_rate = 0.15
gradient_scale = 0.1
parts = 2
group_size = 8


def passed_along(value, axis, by):
    count = lax.axis_size(axis)
    return lax.ppermute(value, axis, [(i, (i + by) % count) for i in range(count)])


def contract(left, right, dims):
    return lax.dot_general(left, right, ((dims[:1], dims[1:]), ((), ())), preferred_element_type=jnp.float32)


def part_kernel(scaling, stratum, part, peak_tiles, load, fresh, *refs):
    count_ref, index_ref, cell_in, peak_in, values_in = refs[:5]
    rest = refs[5:] if fresh else refs[6:]
    new_ref, grad_ref, peak_grad, places = rest[:4]
    own_tiles = peak_tiles // parts
    row_tiles = grad_ref.shape[0] - 1
    live = count_ref[0, stratum]
    slots = index_ref.shape[1]
    if load:
        cell_ref, peak_ref, values_ref, sems = rest[4:]
        copies = [
            pltpu.make_async_copy(peak_in.at[pl.ds(part * own_tiles, own_tiles)], peak_ref, sems.at[0]),
            pltpu.make_async_copy(cell_in, cell_ref, sems.at[1]),
            pltpu.make_async_copy(values_in.at[stratum], values_ref, sems.at[2]),
        ]
        for copy in copies:
            copy.start()
    else:
        cell_ref, peak_ref = cell_in, peak_in
        values_ref = values_in.at[0]

    def note(t, found):
        place = index_ref[stratum, t]
        places[found] = place * slots + t
        mine = (place % peak_tiles) // own_tiles == part
        return found + jnp.where(mine, 1, 0)

    found = lax.fori_loop(0, live, note, 0)
    for k in range(group_size):
        places[found + k] = -1
    peak_grad[...] = jnp.zeros_like(peak_grad)
    grad_ref[...] = jnp.zeros_like(grad_ref) if fresh else refs[5][...]
    if load:
        for copy in copies:
            copy.wait()

    def group(g, carry):
        rows, cols, to_rows, to_cols, lefts, rights, resids = [], [], [], [], [], [], []
        for k in range(group_size):
            code = places[g * group_size + k]
            used = code >= 0
            code = jnp.maximum(code, 0)
            t = code % slots
            place = code // slots
            row = place // peak_tiles
            col = place % own_tiles
            left, right = cell_ref[row], peak_ref[col]
            predicted = contract(left, right, (1, 1))
            resids.append((predicted * scaling - values_ref[t].astype(jnp.float32)).astype(jnp.bfloat16))
            rows.append(row)
            cols.append(col)
            to_rows.append(jnp.where(used, row, row_tiles))
            to_cols.append(jnp.where(used, col, own_tiles))
        terms = [contract(resids[k], cell_ref[rows[k]], (0, 0)) for k in range(group_size)]
        for k in range(group_size):
            peak_grad[to_cols[k]] += terms[k]
        terms = [contract(resids[k], peak_ref[cols[k]], (1, 0)) for k in range(group_size)]
        for k in range(group_size):
            grad_ref[to_rows[k]] += terms[k]
        return carry

    lax.fori_loop(0, (found + group_size - 1) // group_size, group, 0)
    for c in range(own_tiles):
        new_ref[c] = (
            peak_ref[c].astype(jnp.float32) - learning_rate * (peak_grad[c] * scaling)
        ).astype(new_ref.dtype)


def part_update(counts, index, cell_blocks, peaks, values, grad, stratum, part, peak_tiles, load):
    row_tiles, tile_size, rank_width = cell_blocks.shape
    slots = values.shape[1]
    own_tiles = peak_tiles // parts
    fresh = grad is None
    smem = pl.BlockSpec(memory_space=pltpu.SMEM)
    vmem = pl.BlockSpec(memory_space=pltpu.VMEM)
    far = pl.BlockSpec(memory_space=pltpu.HBM)
    if load:
        in_specs = [smem, smem, far, far, far]
    else:
        own_values = pl.BlockSpec((1,) + values.shape[1:], lambda i: (stratum, 0, 0, 0))
        in_specs = [smem, smem, vmem, vmem, own_values]
    args = [counts, index, cell_blocks, peaks, values]
    if not fresh:
        in_specs.append(vmem)
        args.append(grad)
    scratch = [
        pltpu.VMEM((own_tiles + 1, tile_size, rank_width), jnp.float32),
        pltpu.SMEM((slots + group_size,), jnp.int32),
    ]
    if load:
        scratch += [
            pltpu.VMEM(cell_blocks.shape, cell_blocks.dtype),
            pltpu.VMEM((own_tiles, tile_size, rank_width), peaks.dtype),
            pltpu.VMEM(values.shape[1:], values.dtype),
            pltpu.SemaphoreType.DMA((3,)),
        ]
    flops = 6 * slots * tile_size * tile_size * rank_width // parts
    return pl.pallas_call(
        functools.partial(
            part_kernel, 1.0 / math.sqrt(rank_width), stratum, part, peak_tiles, load, fresh
        ),
        grid=(1,),
        out_shape=(
            jax.ShapeDtypeStruct((own_tiles, tile_size, rank_width), peaks.dtype),
            jax.ShapeDtypeStruct((row_tiles + 1, tile_size, rank_width), jnp.float32),
        ),
        in_specs=in_specs,
        out_specs=(vmem, vmem),
        scratch_shapes=scratch,
        compiler_params=pltpu.CompilerParams(vmem_limit_bytes=(60 if load else 12) * 1024 * 1024),
        cost_estimate=pl.CostEstimate(flops=flops, bytes_accessed=4 << 20, transcendentals=0),
    )(*args)


def per_device(cell_factors, peak_factors, tile_values, tile_index, tile_counts):
    cell_dev, rank_width = cell_factors.shape
    tile_size = tile_values.shape[-1]
    strata = tile_values.shape[0]
    block_rows = peak_factors.shape[0]
    row_tiles = cell_dev // tile_size
    peak_tiles = block_rows // tile_size
    chroms = lax.axis_size("chrom")
    share_rows = cell_dev // chroms
    cell_blocks = cell_factors.reshape(row_tiles, tile_size, rank_width)
    peak_block = peak_factors.reshape(peak_tiles, tile_size, rank_width)
    counts = tile_counts.T
    pieces = [peak_block] * parts
    grad = None
    for stratum in range(strata):
        for part in range(parts):
            piece, grad = part_update(
                counts, tile_index, cell_blocks, pieces[part], tile_values, grad,
                stratum, part, peak_tiles, stratum == 0,
            )
            by = -1 if stratum < strata - 1 else strata - 1
            pieces[part] = passed_along(piece, "cell", by)
    scale = gradient_scale / math.sqrt(rank_width)
    local_sum = (grad[:row_tiles].reshape(cell_dev, rank_width) * scale).astype(jnp.bfloat16)
    shares = lax.all_to_all(local_sum, "chrom", 0, 0, tiled=True)
    peak_out = jnp.concatenate(pieces, axis=0)
    peak_out, shares = lax.optimization_barrier((peak_out, shares))
    summed = jnp.sum(shares.reshape(chroms, share_rows, rank_width).astype(jnp.float32), axis=0)
    return (peak_out.reshape(block_rows, rank_width), summed)


def solution(mesh):
    in_specs = (
        P("cell", None),
        P(("cell", "chrom"), None),
        P("cell", "chrom", None, None),
        P("cell", "chrom"),
        P("cell", "chrom"),
    )
    out_specs = (P(("cell", "chrom"), None), P(("cell", "chrom"), None))
    return jax.shard_map(
        per_device, mesh=mesh, in_specs=in_specs, out_specs=out_specs, check_vma=False
    )
```

```python
import functools
import math

import jax
import jax.numpy as jnp
from jax import lax
from jax.experimental import pallas as pl
from jax.experimental.pallas import tpu as pltpu
from jax.sharding import PartitionSpec as P

learning_rate = 0.15
gradient_scale = 0.1
parts = 2
group_size = 8
lanes = 128
mebi = 1024 * 1024

smem = pl.BlockSpec(memory_space=pltpu.SMEM)
vmem = pl.BlockSpec(memory_space=pltpu.VMEM)
far = pl.BlockSpec(memory_space=pltpu.HBM)


def contract(left, right, dims):
    return lax.dot_general(left, right, ((dims[:1], dims[1:]), ((), ())), preferred_element_type=jnp.float32)


def walk(groups, slot_of, cell_ref, peak_ref, values_at, peak_grad, grad_ref, scaling):
    def group(g, carry):
        found = [slot_of(g * group_size + k) for k in range(group_size)]
        resids = []
        for t, row, col, _, _ in found:
            predicted = contract(cell_ref[row], peak_ref[col], (1, 1))
            resids.append((predicted * scaling - values_at(t).astype(jnp.float32)).astype(jnp.bfloat16))
        terms = [contract(r, cell_ref[f[1]], (0, 0)) for r, f in zip(resids, found)]
        for term, f in zip(terms, found):
            peak_grad[f[4]] += term
        terms = [contract(r, peak_ref[f[2]], (1, 0)) for r, f in zip(resids, found)]
        for term, f in zip(terms, found):
            grad_ref[f[3]] += term
        return carry

    lax.fori_loop(0, groups, group, 0)


def stepped(peak, grad, scaling):
    return (peak.astype(jnp.float32) - learning_rate * (grad * scaling)).astype(jnp.bfloat16)


def first_kernel(scaling, last, counts, index, cell_in, peak_in, values_in, *refs):
    news, (grad_ref, pack, cell_ref, peak_ref, values_ref, meta, peak_grad, sems) = refs[:parts], refs[parts:]
    row_tiles, tile_size, _ = cell_ref.shape
    peak_tiles = peak_ref.shape[0]
    slots = values_ref.shape[0]
    loads = [
        pltpu.make_async_copy(cell_in, cell_ref, sems.at[0]),
        pltpu.make_async_copy(peak_in, peak_ref, sems.at[1]),
        pltpu.make_async_copy(values_in.at[0], values_ref, sems.at[2]),
    ]
    for copy in loads:
        copy.start()
    lane = lax.broadcasted_iota(jnp.int32, (tile_size, lanes), 1)
    coded = jnp.full((tile_size, lanes), counts[0, last], jnp.int32)
    for t in range(slots):
        coded = jnp.where(lane == t, index[last, t], coded)
    meta[...] = coded.astype(jnp.float32).astype(meta.dtype)
    sends = [
        pltpu.make_async_copy(cell_in, pack.at[pl.ds(0, row_tiles)], sems.at[3]),
        pltpu.make_async_copy(meta, pack.at[row_tiles, :, pl.ds(0, lanes)], sems.at[4]),
        pltpu.make_async_copy(meta, pack.at[row_tiles, :, pl.ds(lanes, lanes)], sems.at[5]),
    ]
    for t in range(slots):
        place = pack.at[row_tiles + 1 + t // 2, :, pl.ds((t % 2) * lanes, lanes)]
        sends.append(pltpu.make_async_copy(values_in.at[last, t], place, sems.at[6 + t]))
    for copy in sends:
        copy.start()
    peak_grad[...] = jnp.zeros_like(peak_grad)
    grad_ref[...] = jnp.zeros_like(grad_ref)
    for copy in loads:
        copy.wait()

    def slot_of(t):
        place = index[0, t]
        row, col = place // peak_tiles, place % peak_tiles
        return t, row, col, row, col

    groups = counts[0, 0] // group_size
    walk(groups, slot_of, cell_ref, peak_ref, lambda t: values_ref[t], peak_grad, grad_ref, scaling)
    own_tiles = peak_tiles // parts
    for c in range(peak_tiles):
        news[c // own_tiles][c % own_tiles] = stepped(peak_ref[c], peak_grad[c], scaling)
    for copy in sends:
        copy.wait()


def part_kernel(scaling, stratum, part, peak_tiles, packed, closing, fresh, *refs):
    if packed:
        meta, pack, peak_ref, *rest = refs
        cell_ref = pack
    else:
        counts, index, cell_ref, values, peak_ref, *rest = refs
    given = None
    if not fresh:
        given, *rest = rest
    if closing:
        early, new_ref, out_ref, grad_ref, peak_grad, places = rest
    else:
        new_ref, grad_ref, peak_grad, places = rest
    own_tiles = peak_ref.shape[0]
    row_tiles = grad_ref.shape[0] - 1
    slots = places.shape[0] - group_size
    live = meta[0, slots] if packed else counts[0, stratum]
    placed = (lambda t: meta[0, t]) if packed else (lambda t: index[stratum, t])

    def values_at(t):
        if not packed:
            return values[0, t]
        column = pl.multiple_of((t % 2) * lanes, lanes)
        return pack[row_tiles + 1 + t // 2, :, pl.ds(column, lanes)]

    def note(t, found):
        place = placed(t)
        places[found] = place * slots + t
        mine = (place % peak_tiles) // own_tiles == part
        return found + jnp.where(mine, 1, 0)

    found = lax.fori_loop(0, live, note, 0)
    for k in range(group_size):
        places[found + k] = -1
    peak_grad[...] = jnp.zeros_like(peak_grad)
    grad_ref[...] = jnp.zeros_like(grad_ref) if fresh else given[...]

    def slot_of(k):
        code = places[k]
        used = code >= 0
        code = jnp.maximum(code, 0)
        place = code // slots
        row, col = place // peak_tiles, place % own_tiles
        return code % slots, row, col, jnp.where(used, row, row_tiles), jnp.where(used, col, own_tiles)

    groups = (found + group_size - 1) // group_size
    walk(groups, slot_of, cell_ref, peak_ref, values_at, peak_grad, grad_ref, scaling)
    for c in range(own_tiles):
        new_ref[c] = stepped(peak_ref[c], peak_grad[c], scaling)
    if closing:
        for r in range(row_tiles):
            out_ref[r, 0] = (early[r] * (gradient_scale * scaling)).astype(out_ref.dtype)
            out_ref[r, 1] = (grad_ref[r] * (gradient_scale * scaling)).astype(out_ref.dtype)


def last_kernel(scaling, *refs):
    pieces, (shares, late, out_ref, sum_ref, sems) = refs[:parts], refs[parts:]
    own_tiles = pieces[0].shape[0]
    copies = [
        pltpu.make_async_copy(pieces[p], out_ref.at[pl.ds(p * own_tiles, own_tiles)], sems.at[p])
        for p in range(parts)
    ]
    for copy in copies:
        copy.start()
    total = late[...].astype(jnp.float32)
    for j in range(shares.shape[0]):
        total = total + shares[j, 0].astype(jnp.float32)
    sum_ref[...] = total
    for copy in copies:
        copy.wait()


def cost(flops, read):
    return pl.CostEstimate(flops=flops, bytes_accessed=read, transcendentals=0)


def per_device(cell_factors, peak_factors, tile_values, tile_index, tile_counts):
    cell_dev, rank_width = cell_factors.shape
    strata, slots, tile_size, _ = tile_values.shape
    block_rows = peak_factors.shape[0]
    row_tiles = cell_dev // tile_size
    peak_tiles = block_rows // tile_size
    own_tiles = peak_tiles // parts
    chroms = lax.axis_size("chrom")
    cells = lax.axis_size("cell")
    share_rows = cell_dev // chroms
    scaling = 1.0 / math.sqrt(rank_width)
    flops = 6 * slots * tile_size * tile_size * rank_width
    cell_blocks = cell_factors.reshape(row_tiles, tile_size, rank_width)
    peak_block = peak_factors.reshape(peak_tiles, tile_size, rank_width)
    counts = tile_counts.T
    last = strata - 1
    grid_spec = dict(grid=(1,))

    back_one = [(i, (i - 1) % cells) for i in range(cells)]
    swap = [(i, i ^ 1) for i in range(cells)]
    odd_on = [(i, (i + 2) % cells if i % 2 else i) for i in range(cells)]
    odd_back = [(i, (i - 2) % cells if i % 2 else i) for i in range(cells)]
    even_on = [(i, i if i % 2 else (i + 2) % cells) for i in range(cells)]

    piece_shape = (own_tiles, tile_size, rank_width)
    piece_out = jax.ShapeDtypeStruct(piece_shape, jnp.bfloat16)
    grad_out = jax.ShapeDtypeStruct((row_tiles + 1, tile_size, rank_width), jnp.float32)
    pack_out = jax.ShapeDtypeStruct((row_tiles + 1 + slots // 2, tile_size, rank_width), jnp.bfloat16)

    *pieces, grad, pack = pl.pallas_call(
        functools.partial(first_kernel, scaling, last),
        out_shape=(piece_out,) * parts + (grad_out, pack_out),
        in_specs=[smem, smem, far, far, far],
        out_specs=(vmem,) * parts + (vmem, far),
        scratch_shapes=[
            pltpu.VMEM(cell_blocks.shape, jnp.bfloat16),
            pltpu.VMEM(peak_block.shape, jnp.bfloat16),
            pltpu.VMEM(tile_values.shape[1:], jnp.bfloat16),
            pltpu.VMEM((tile_size, lanes), jnp.bfloat16),
            pltpu.VMEM(peak_block.shape, jnp.float32),
            pltpu.SemaphoreType.DMA((6 + slots,)),
        ],
        compiler_params=pltpu.CompilerParams(vmem_limit_bytes=60 * mebi),
        cost_estimate=cost(flops, 8 * mebi),
        **grid_spec,
    )(counts, tile_index, cell_blocks, peak_block, tile_values)
    pieces = [lax.ppermute(piece, "cell", back_one) for piece in pieces]
    pack = lax.ppermute(pack, "cell", odd_on)
    meta = pack[row_tiles, :1, :lanes].astype(jnp.int32)

    def part_call(stratum, part, piece, given, early):
        packed = stratum == last
        closing = early is not None
        if packed:
            args, in_specs = [meta, pack, piece], [smem, vmem, vmem]
        else:
            own_values = pl.BlockSpec((1,) + tile_values.shape[1:], lambda i: (stratum, 0, 0, 0))
            args = [counts, tile_index, cell_blocks, tile_values, piece]
            in_specs = [smem, smem, vmem, own_values, vmem]
        if given is not None:
            args.append(given)
        if closing:
            args.append(early)
        in_specs += [vmem] * (len(args) - len(in_specs))
        scratch = [
            pltpu.VMEM((own_tiles + 1, tile_size, rank_width), jnp.float32),
            pltpu.SMEM((slots + group_size,), jnp.int32),
        ]
        if closing:
            out_shape = (piece_out, jax.ShapeDtypeStruct((row_tiles, 2, tile_size, rank_width), jnp.bfloat16))
            scratch.insert(0, pltpu.VMEM(grad_out.shape, jnp.float32))
        else:
            out_shape = (piece_out, grad_out)
        return pl.pallas_call(
            functools.partial(
                part_kernel, scaling, stratum, part, peak_tiles, packed, closing, given is None
            ),
            out_shape=out_shape,
            in_specs=in_specs,
            out_specs=(vmem, vmem),
            scratch_shapes=scratch,
            compiler_params=pltpu.CompilerParams(vmem_limit_bytes=16 * mebi),
            cost_estimate=cost(flops // parts, 3 * mebi),
            **grid_spec,
        )(*args)

    for part in range(parts):
        pieces[part], grad = part_call(1, part, pieces[part], grad, None)
        pieces[part] = lax.ppermute(pieces[part], "cell", swap)
    early, late = grad, None
    for part in range(parts):
        pieces[part], late = part_call(
            last, part, pieces[part], late, early if part == parts - 1 else None
        )
        pieces[part] = lax.ppermute(pieces[part], "cell", even_on)
    shares = late.reshape(chroms, cell_dev // chroms // tile_size, 2, tile_size, rank_width)
    shares = shares.transpose(0, 2, 1, 3, 4).reshape(chroms, 2, share_rows, rank_width)
    shares = lax.all_to_all(shares, "chrom", 0, 0, tiled=True)
    owed = jnp.sum(shares[:, 1].astype(jnp.float32), axis=0).astype(jnp.bfloat16)
    owed = lax.ppermute(owed, "cell", odd_back)
    peak_out, summed = pl.pallas_call(
        functools.partial(last_kernel, scaling),
        out_shape=(
            jax.ShapeDtypeStruct(peak_block.shape, jnp.bfloat16),
            jax.ShapeDtypeStruct((share_rows, rank_width), jnp.float32),
        ),
        in_specs=[vmem] * (parts + 2),
        out_specs=(far, vmem),
        scratch_shapes=[pltpu.SemaphoreType.DMA((parts,))],
        compiler_params=pltpu.CompilerParams(vmem_limit_bytes=16 * mebi),
        cost_estimate=cost(0, 3 * mebi),
        **grid_spec,
    )(*pieces, shares, owed)
    return (peak_out.reshape(block_rows, rank_width), summed)


def solution(mesh):
    in_specs = (
        P("cell", None),
        P(("cell", "chrom"), None),
        P("cell", "chrom", None, None),
        P("cell", "chrom"),
        P("cell", "chrom"),
    )
    out_specs = (P(("cell", "chrom"), None), P(("cell", "chrom"), None))
    return jax.shard_map(
        per_device, mesh=mesh, in_specs=in_specs, out_specs=out_specs, check_vma=False
    )
```

```python
import functools
import math

import jax
import jax.numpy as jnp
from jax import lax
from jax.experimental import pallas as pl
from jax.experimental.pallas import tpu as pltpu
from jax.sharding import PartitionSpec as P

learning_rate = 0.15
gradient_scale = 0.1
parts = 2
group_size = 8
lanes = 128
mebi = 1024 * 1024

smem = pl.BlockSpec(memory_space=pltpu.SMEM)
vmem = pl.BlockSpec(memory_space=pltpu.VMEM)
far = pl.BlockSpec(memory_space=pltpu.HBM)


def contract(left, right, dims):
    return lax.dot_general(left, right, ((dims[:1], dims[1:]), ((), ())), preferred_element_type=jnp.float32)


def walk(groups, slot_of, cell_ref, peak_ref, values_at, peak_grad, grad_ref, scaling):
    def group(g, carry):
        found = [slot_of(g * group_size + k) for k in range(group_size)]
        resids = []
        for t, row, col, _, _ in found:
            predicted = contract(cell_ref[row], peak_ref[col], (1, 1))
            resids.append((predicted * scaling - values_at(t).astype(jnp.float32)).astype(jnp.bfloat16))
        terms = [contract(r, cell_ref[f[1]], (0, 0)) for r, f in zip(resids, found)]
        for term, f in zip(terms, found):
            peak_grad[f[4]] += term
        terms = [contract(r, peak_ref[f[2]], (1, 0)) for r, f in zip(resids, found)]
        for term, f in zip(terms, found):
            grad_ref[f[3]] += term
        return carry

    lax.fori_loop(0, groups, group, 0)


def stepped(peak, grad, scaling):
    return (peak.astype(jnp.float32) - learning_rate * (grad * scaling)).astype(jnp.bfloat16)


def first_kernel(scaling, counts, index, cell_in, peak_in, values_in, *refs):
    news, (grad_ref, cell_ref, peak_ref, values_ref, peak_grad, sems) = refs[:parts], refs[parts:]
    peak_tiles = peak_ref.shape[0]
    loads = [
        pltpu.make_async_copy(cell_in, cell_ref, sems.at[0]),
        pltpu.make_async_copy(peak_in, peak_ref, sems.at[1]),
        pltpu.make_async_copy(values_in.at[0], values_ref, sems.at[2]),
    ]
    for copy in loads:
        copy.start()
    peak_grad[...] = jnp.zeros_like(peak_grad)
    grad_ref[...] = jnp.zeros_like(grad_ref)
    for copy in loads:
        copy.wait()

    def slot_of(t):
        place = index[0, t]
        row, col = place // peak_tiles, place % peak_tiles
        return t, row, col, row, col

    groups = counts[0, 0] // group_size
    walk(groups, slot_of, cell_ref, peak_ref, lambda t: values_ref[t], peak_grad, grad_ref, scaling)
    own_tiles = peak_tiles // parts
    for c in range(peak_tiles):
        news[c // own_tiles][c % own_tiles] = stepped(peak_ref[c], peak_grad[c], scaling)


def part_kernel(scaling, stratum, part, peak_tiles, closing, fresh, *refs):
    counts, index, cell_ref, values, peak_ref, *rest = refs
    given = None
    if not fresh:
        given, *rest = rest
    if closing:
        early, new_ref, out_ref, grad_ref, peak_grad, places = rest
    else:
        new_ref, grad_ref, peak_grad, places = rest
    own_tiles = peak_ref.shape[0]
    row_tiles = grad_ref.shape[0] - 1
    slots = places.shape[0] - group_size

    def note(t, found):
        place = index[stratum, t]
        places[found] = place * slots + t
        mine = (place % peak_tiles) // own_tiles == part
        return found + jnp.where(mine, 1, 0)

    found = lax.fori_loop(0, counts[0, stratum], note, 0)
    for k in range(group_size):
        places[found + k] = -1
    peak_grad[...] = jnp.zeros_like(peak_grad)
    grad_ref[...] = jnp.zeros_like(grad_ref) if fresh else given[...]

    def slot_of(k):
        code = places[k]
        used = code >= 0
        code = jnp.maximum(code, 0)
        place = code // slots
        row, col = place // peak_tiles, place % own_tiles
        return code % slots, row, col, jnp.where(used, row, row_tiles), jnp.where(used, col, own_tiles)

    groups = (found + group_size - 1) // group_size
    walk(groups, slot_of, cell_ref, peak_ref, lambda t: values[0, t], peak_grad, grad_ref, scaling)
    for c in range(own_tiles):
        new_ref[c] = stepped(peak_ref[c], peak_grad[c], scaling)
    if closing:
        for r in range(row_tiles):
            out_ref[r] = ((early[r] + grad_ref[r]) * (gradient_scale * scaling)).astype(out_ref.dtype)


def place_kernel(*refs):
    pieces, (out_ref, sems) = refs[:parts], refs[parts:]
    own_tiles = pieces[0].shape[0]
    copies = [
        pltpu.make_async_copy(pieces[p], out_ref.at[pl.ds(p * own_tiles, own_tiles)], sems.at[p])
        for p in range(parts)
    ]
    for copy in copies:
        copy.start()
    for copy in copies:
        copy.wait()


def cost(flops, read):
    return pl.CostEstimate(flops=flops, bytes_accessed=read, transcendentals=0)


def per_device(cell_factors, peak_factors, tile_values, tile_index, tile_counts):
    cell_dev, rank_width = cell_factors.shape
    strata, slots, tile_size, _ = tile_values.shape
    block_rows = peak_factors.shape[0]
    row_tiles = cell_dev // tile_size
    peak_tiles = block_rows // tile_size
    own_tiles = peak_tiles // parts
    chroms = lax.axis_size("chrom")
    cells = lax.axis_size("cell")
    share_rows = cell_dev // chroms
    scaling = 1.0 / math.sqrt(rank_width)
    flops = 6 * slots * tile_size * tile_size * rank_width
    cell_blocks = cell_factors.reshape(row_tiles, tile_size, rank_width)
    peak_block = peak_factors.reshape(peak_tiles, tile_size, rank_width)
    counts = tile_counts.T
    last = strata - 1

    def moved(piece, by):
        return lax.ppermute(piece, "cell", [(i, (i + by) % cells) for i in range(cells)])

    piece_out = jax.ShapeDtypeStruct((own_tiles, tile_size, rank_width), jnp.bfloat16)
    grad_out = jax.ShapeDtypeStruct((row_tiles + 1, tile_size, rank_width), jnp.float32)

    *pieces, early = pl.pallas_call(
        functools.partial(first_kernel, scaling),
        grid=(1,),
        out_shape=(piece_out,) * parts + (jax.ShapeDtypeStruct(cell_blocks.shape, jnp.float32),),
        in_specs=[smem, smem, far, far, far],
        out_specs=(vmem,) * (parts + 1),
        scratch_shapes=[
            pltpu.VMEM(cell_blocks.shape, jnp.bfloat16),
            pltpu.VMEM(peak_block.shape, jnp.bfloat16),
            pltpu.VMEM(tile_values.shape[1:], jnp.bfloat16),
            pltpu.VMEM(peak_block.shape, jnp.float32),
            pltpu.SemaphoreType.DMA((3,)),
        ],
        compiler_params=pltpu.CompilerParams(vmem_limit_bytes=60 * mebi),
        cost_estimate=cost(flops, 4 * mebi),
    )(counts, tile_index, cell_blocks, peak_block, tile_values)
    pieces = [moved(piece, -1) for piece in pieces]

    def part_call(stratum, part, piece, given, closing):
        own_values = pl.BlockSpec((1,) + tile_values.shape[1:], lambda i: (stratum, 0, 0, 0))
        args = [counts, tile_index, cell_blocks, tile_values, piece]
        in_specs = [smem, smem, vmem, own_values, vmem]
        if given is not None:
            args.append(given)
        if closing:
            args.append(early)
        in_specs += [vmem] * (len(args) - len(in_specs))
        scratch = [
            pltpu.VMEM((own_tiles + 1, tile_size, rank_width), jnp.float32),
            pltpu.SMEM((slots + group_size,), jnp.int32),
        ]
        second = grad_out
        if closing:
            second = jax.ShapeDtypeStruct(cell_blocks.shape, jnp.bfloat16)
            scratch.insert(0, pltpu.VMEM(grad_out.shape, jnp.float32))
        return pl.pallas_call(
            functools.partial(part_kernel, scaling, stratum, part, peak_tiles, closing, given is None),
            grid=(1,),
            out_shape=(piece_out, second),
            in_specs=in_specs,
            out_specs=(vmem, vmem),
            scratch_shapes=scratch,
            compiler_params=pltpu.CompilerParams(vmem_limit_bytes=16 * mebi),
            cost_estimate=cost(flops // parts, 3 * mebi),
        )(*args)

    grad = None
    for stratum in range(1, strata):
        for part in range(parts):
            closing = stratum == last and part == parts - 1
            piece, grad = part_call(stratum, part, pieces[part], grad, closing)
            pieces[part] = moved(piece, last if stratum == last else -1)
    shares = lax.all_to_all(grad.reshape(cell_dev, rank_width), "chrom", 0, 0, tiled=True)
    peak_out = pl.pallas_call(
        place_kernel,
        grid=(1,),
        out_shape=jax.ShapeDtypeStruct(peak_block.shape, jnp.bfloat16),
        in_specs=[vmem] * parts,
        out_specs=far,
        scratch_shapes=[pltpu.SemaphoreType.DMA((parts,))],
        compiler_params=pltpu.CompilerParams(vmem_limit_bytes=16 * mebi),
        cost_estimate=cost(0, 8 * mebi),
    )(*pieces)
    peak_out, shares = lax.optimization_barrier((peak_out, shares))
    summed = jnp.sum(shares.reshape(chroms, share_rows, rank_width).astype(jnp.float32), axis=0)
    return (peak_out.reshape(block_rows, rank_width), summed)


def solution(mesh):
    in_specs = (
        P("cell", None),
        P(("cell", "chrom"), None),
        P("cell", "chrom", None, None),
        P("cell", "chrom"),
        P("cell", "chrom"),
    )
    out_specs = (P(("cell", "chrom"), None), P(("cell", "chrom"), None))
    return jax.shard_map(
        per_device, mesh=mesh, in_specs=in_specs, out_specs=out_specs, check_vma=False
    )
```

```python
import functools
import math

import jax
import jax.numpy as jnp
from jax import lax
from jax.experimental import pallas as pl
from jax.experimental.pallas import tpu as pltpu
from jax.sharding import PartitionSpec as P

learning_rate = 0.15
gradient_scale = 0.1
parts = 2
group_size = 8
lanes = 128
mebi = 1024 * 1024

smem = pl.BlockSpec(memory_space=pltpu.SMEM)
vmem = pl.BlockSpec(memory_space=pltpu.VMEM)
far = pl.BlockSpec(memory_space=pltpu.HBM)


def contract(left, right, dims):
    return lax.dot_general(left, right, ((dims[:1], dims[1:]), ((), ())), preferred_element_type=jnp.float32)


def walk(groups, slot_of, cell_ref, peak_ref, values_at, peak_grad, grad_ref, scaling):
    def group(g, carry):
        found = [slot_of(g * group_size + k) for k in range(group_size)]
        resids = []
        for t, row, col, _, _ in found:
            predicted = contract(cell_ref[row], peak_ref[col], (1, 1))
            resids.append((predicted * scaling - values_at(t).astype(jnp.float32)).astype(jnp.bfloat16))
        terms = [contract(r, cell_ref[f[1]], (0, 0)) for r, f in zip(resids, found)]
        for term, f in zip(terms, found):
            peak_grad[f[4]] += term
        terms = [contract(r, peak_ref[f[2]], (1, 0)) for r, f in zip(resids, found)]
        for term, f in zip(terms, found):
            grad_ref[f[3]] += term
        return carry

    lax.fori_loop(0, groups, group, 0)


def stepped(peak, grad, scaling):
    return (peak.astype(jnp.float32) - learning_rate * (grad * scaling)).astype(jnp.bfloat16)


def first_kernel(scaling, counts, index, cell_in, peak_in, values_in, *refs):
    news, (grad_ref, cell_ref, peak_ref, values_ref, peak_grad, sems) = refs[:parts], refs[parts:]
    peak_tiles = peak_ref.shape[0]
    loads = [
        pltpu.make_async_copy(cell_in, cell_ref, sems.at[0]),
        pltpu.make_async_copy(peak_in, peak_ref, sems.at[1]),
        pltpu.make_async_copy(values_in.at[0], values_ref, sems.at[2]),
    ]
    for copy in loads:
        copy.start()
    peak_grad[...] = jnp.zeros_like(peak_grad)
    grad_ref[...] = jnp.zeros_like(grad_ref)
    for copy in loads:
        copy.wait()

    def slot_of(t):
        place = index[0, t]
        row, col = place // peak_tiles, place % peak_tiles
        return t, row, col, row, col

    groups = counts[0, 0] // group_size
    walk(groups, slot_of, cell_ref, peak_ref, lambda t: values_ref[t], peak_grad, grad_ref, scaling)
    own_tiles = peak_tiles // parts
    for c in range(peak_tiles):
        news[c // own_tiles][c % own_tiles] = stepped(peak_ref[c], peak_grad[c], scaling)


def part_kernel(scaling, stratum, part, peak_tiles, closing, fresh, *refs):
    counts, index, cell_ref, values, peak_ref, *rest = refs
    given = None
    if not fresh:
        given, *rest = rest
    if closing:
        early, new_ref, out_ref, grad_ref, peak_grad, places = rest
    else:
        new_ref, grad_ref, peak_grad, places = rest
    own_tiles = peak_ref.shape[0]
    row_tiles = grad_ref.shape[0] - 1
    slots = places.shape[0] - group_size

    def note(t, found):
        place = index[stratum, t]
        places[found] = place * slots + t
        mine = (place % peak_tiles) // own_tiles == part
        return found + jnp.where(mine, 1, 0)

    found = lax.fori_loop(0, counts[0, stratum], note, 0)
    for k in range(group_size):
        places[found + k] = -1
    peak_grad[...] = jnp.zeros_like(peak_grad)
    grad_ref[...] = jnp.zeros_like(grad_ref) if fresh else given[...]

    def slot_of(k):
        code = places[k]
        used = code >= 0
        code = jnp.maximum(code, 0)
        place = code // slots
        row, col = place // peak_tiles, place % own_tiles
        return code % slots, row, col, jnp.where(used, row, row_tiles), jnp.where(used, col, own_tiles)

    groups = (found + group_size - 1) // group_size
    walk(groups, slot_of, cell_ref, peak_ref, lambda t: values[0, t], peak_grad, grad_ref, scaling)
    for c in range(own_tiles):
        new_ref[c] = stepped(peak_ref[c], peak_grad[c], scaling)
    if closing:
        near = out_ref.shape[0]
        for r in range(row_tiles):
            out_ref[r % near, r // near] = ((early[r] + grad_ref[r]) * (gradient_scale * scaling)).astype(out_ref.dtype)


def place_kernel(part, piece_ref, *refs):
    out_ref, sem = refs[-2:]
    own_tiles = piece_ref.shape[0]
    copy = pltpu.make_async_copy(piece_ref, out_ref.at[pl.ds(part * own_tiles, own_tiles)], sem)
    copy.start()
    copy.wait()


def cost(flops, read):
    return pl.CostEstimate(flops=flops, bytes_accessed=read, transcendentals=0)


def per_device(cell_factors, peak_factors, tile_values, tile_index, tile_counts):
    cell_dev, rank_width = cell_factors.shape
    strata, slots, tile_size, _ = tile_values.shape
    block_rows = peak_factors.shape[0]
    row_tiles = cell_dev // tile_size
    peak_tiles = block_rows // tile_size
    own_tiles = peak_tiles // parts
    chroms = lax.axis_size("chrom")
    cells = lax.axis_size("cell")
    share_rows = cell_dev // chroms
    assert share_rows == tile_size
    near = chroms // 2
    scaling = 1.0 / math.sqrt(rank_width)
    flops = 6 * slots * tile_size * tile_size * rank_width
    cell_blocks = cell_factors.reshape(row_tiles, tile_size, rank_width)
    peak_block = peak_factors.reshape(peak_tiles, tile_size, rank_width)
    counts = tile_counts.T
    last = strata - 1

    def moved(piece, by):
        return lax.ppermute(piece, "cell", [(i, (i + by) % cells) for i in range(cells)])

    piece_out = jax.ShapeDtypeStruct((own_tiles, tile_size, rank_width), jnp.bfloat16)
    grad_out = jax.ShapeDtypeStruct((row_tiles + 1, tile_size, rank_width), jnp.float32)

    *pieces, early = pl.pallas_call(
        functools.partial(first_kernel, scaling),
        grid=(1,),
        out_shape=(piece_out,) * parts + (jax.ShapeDtypeStruct(cell_blocks.shape, jnp.float32),),
        in_specs=[smem, smem, far, far, far],
        out_specs=(vmem,) * (parts + 1),
        scratch_shapes=[
            pltpu.VMEM(cell_blocks.shape, jnp.bfloat16),
            pltpu.VMEM(peak_block.shape, jnp.bfloat16),
            pltpu.VMEM(tile_values.shape[1:], jnp.bfloat16),
            pltpu.VMEM(peak_block.shape, jnp.float32),
            pltpu.SemaphoreType.DMA((3,)),
        ],
        compiler_params=pltpu.CompilerParams(vmem_limit_bytes=60 * mebi),
        cost_estimate=cost(flops, 4 * mebi),
    )(counts, tile_index, cell_blocks, peak_block, tile_values)
    pieces = [moved(piece, -1) for piece in pieces]

    def part_call(stratum, part, piece, given, closing):
        own_values = pl.BlockSpec((1,) + tile_values.shape[1:], lambda i: (stratum, 0, 0, 0))
        args = [counts, tile_index, cell_blocks, tile_values, piece]
        in_specs = [smem, smem, vmem, own_values, vmem]
        if given is not None:
            args.append(given)
        if closing:
            args.append(early)
        in_specs += [vmem] * (len(args) - len(in_specs))
        scratch = [
            pltpu.VMEM((own_tiles + 1, tile_size, rank_width), jnp.float32),
            pltpu.SMEM((slots + group_size,), jnp.int32),
        ]
        second = grad_out
        if closing:
            second = jax.ShapeDtypeStruct((near, chroms // near, share_rows, rank_width), jnp.bfloat16)
            scratch.insert(0, pltpu.VMEM(grad_out.shape, jnp.float32))
        return pl.pallas_call(
            functools.partial(part_kernel, scaling, stratum, part, peak_tiles, closing, given is None),
            grid=(1,),
            out_shape=(piece_out, second),
            in_specs=in_specs,
            out_specs=(vmem, vmem),
            scratch_shapes=scratch,
            compiler_params=pltpu.CompilerParams(vmem_limit_bytes=16 * mebi),
            cost_estimate=cost(flops // parts, 3 * mebi),
        )(*args)

    grad = None
    for stratum in range(1, strata):
        for part in range(parts):
            closing = stratum == last and part == parts - 1
            piece, grad = part_call(stratum, part, pieces[part], grad, closing)
            pieces[part] = moved(piece, last if stratum == last else -1)

    def put(part, peak_out):
        args = [pieces[part]] + ([] if peak_out is None else [peak_out])
        return pl.pallas_call(
            functools.partial(place_kernel, part),
            grid=(1,),
            out_shape=jax.ShapeDtypeStruct(peak_block.shape, jnp.bfloat16),
            in_specs=[vmem, far][: len(args)],
            out_specs=far,
            scratch_shapes=[pltpu.SemaphoreType.DMA],
            input_output_aliases={} if peak_out is None else {1: 0},
            compiler_params=pltpu.CompilerParams(vmem_limit_bytes=16 * mebi),
            cost_estimate=cost(0, 8 * mebi),
        )(*args)

    rings = [list(range(r * near, (r + 1) * near)) for r in range(chroms // near)]
    shares = lax.all_to_all(grad, "chrom", 0, 0, axis_index_groups=rings, tiled=True)
    peak_out = None
    for part in range(parts - 1):
        peak_out = put(part, peak_out)
    peak_out, shares = lax.optimization_barrier((peak_out, shares))
    shares = jnp.sum(shares.astype(jnp.float32), axis=0)
    side = lax.axis_index("chrom") // near
    kept = lax.dynamic_index_in_dim(shares, side, 0, keepdims=False)
    sent = lax.dynamic_index_in_dim(shares, 1 - side, 0, keepdims=False).astype(jnp.bfloat16)
    got = lax.ppermute(sent, "chrom", [(j, (j + near) % chroms) for j in range(chroms)])
    peak_out = put(parts - 1, peak_out)
    peak_out, got = lax.optimization_barrier((peak_out, got))
    summed = kept + got.astype(jnp.float32)
    return (peak_out.reshape(block_rows, rank_width), summed)


def solution(mesh):
    in_specs = (
        P("cell", None),
        P(("cell", "chrom"), None),
        P("cell", "chrom", None, None),
        P("cell", "chrom"),
        P("cell", "chrom"),
    )
    out_specs = (P(("cell", "chrom"), None), P(("cell", "chrom"), None))
    return jax.shard_map(
        per_device, mesh=mesh, in_specs=in_specs, out_specs=out_specs, check_vma=False
    )
```

```python
import functools
import math

import jax
import jax.numpy as jnp
from jax import lax
from jax.experimental import pallas as pl
from jax.experimental.pallas import tpu as pltpu
from jax.sharding import PartitionSpec as P

learning_rate = 0.15
gradient_scale = 0.1
parts = 2
group_size = 8
lanes = 128
mebi = 1024 * 1024

smem = pl.BlockSpec(memory_space=pltpu.SMEM)
vmem = pl.BlockSpec(memory_space=pltpu.VMEM)
far = pl.BlockSpec(memory_space=pltpu.HBM)


def contract(left, right, dims):
    return lax.dot_general(left, right, ((dims[:1], dims[1:]), ((), ())), preferred_element_type=jnp.float32)


def walk(groups, slot_of, cell_ref, peak_ref, values_at, peak_grad, grad_ref, scaling):
    def group(g, carry):
        found = [slot_of(g * group_size + k) for k in range(group_size)]
        resids = []
        for t, row, col, _, _ in found:
            predicted = contract(cell_ref[row], peak_ref[col], (1, 1))
            resids.append((predicted * scaling - values_at(t).astype(jnp.float32)).astype(jnp.bfloat16))
        terms = [contract(r, cell_ref[f[1]], (0, 0)) for r, f in zip(resids, found)]
        for term, f in zip(terms, found):
            peak_grad[f[4]] += term
        terms = [contract(r, peak_ref[f[2]], (1, 0)) for r, f in zip(resids, found)]
        for term, f in zip(terms, found):
            grad_ref[f[3]] += term
        return carry

    lax.fori_loop(0, groups, group, 0)


def stepped(peak, grad, scaling):
    return (peak.astype(jnp.float32) - learning_rate * (grad * scaling)).astype(jnp.bfloat16)


def spread(found_ref, index, stratum, live, part, own_tiles, peak_tiles, slots):
    def note(t, found):
        place = index[stratum, t]
        found_ref[found] = place * slots + t
        mine = (place % peak_tiles) // own_tiles == part
        return found + jnp.where(mine, 1, 0)

    found = lax.fori_loop(0, live, note, 0)
    for k in range(group_size):
        found_ref[found + k] = -1
    return (found + group_size - 1) // group_size


def slot_at(found_ref, k, slots, row_tiles, own_tiles, peak_tiles):
    code = found_ref[k]
    used = code >= 0
    code = jnp.maximum(code, 0)
    place = code // slots
    row, col = place // peak_tiles, place % own_tiles
    return code % slots, row, col, jnp.where(used, row, row_tiles), jnp.where(used, col, own_tiles)


def first_kernel(scaling, part, peak_tiles, counts, index, cell_in, peak_in, values_in, *refs):
    new_ref, grad_ref, cell_ref, peak_ref, values_ref, peak_grad, found_ref, sems = refs[-8:]
    own_tiles = peak_ref.shape[0]
    row_tiles = cell_ref.shape[0]
    slots = values_ref.shape[0]
    loads = [
        pltpu.make_async_copy(cell_in, cell_ref, sems.at[0]),
        pltpu.make_async_copy(peak_in.at[pl.ds(part * own_tiles, own_tiles)], peak_ref, sems.at[1]),
        pltpu.make_async_copy(values_in.at[0], values_ref, sems.at[2]),
    ]
    for copy in loads:
        copy.start()
    groups = spread(found_ref, index, 0, counts[0, 0], part, own_tiles, peak_tiles, slots)
    peak_grad[...] = jnp.zeros_like(peak_grad)
    grad_ref[...] = jnp.zeros_like(grad_ref)
    for copy in loads:
        copy.wait()
    slot_of = lambda k: slot_at(found_ref, k, slots, row_tiles, own_tiles, peak_tiles)
    walk(groups, slot_of, cell_ref, peak_ref, lambda t: values_ref[t], peak_grad, grad_ref, scaling)
    for c in range(own_tiles):
        new_ref[c] = stepped(peak_ref[c], peak_grad[c], scaling)


def part_kernel(scaling, stratum, part, parity, peak_tiles, closing, fresh, *refs):
    counts, index, cell_ref, values, peak_ref, *rest = refs
    if not fresh:
        given, *rest = rest
    if closing:
        *earlier, other, new_ref, out_ref, grad_ref, peak_grad, found_ref = rest[1:]
    else:
        new_ref, grad_ref, _, peak_grad, found_ref = rest[-5:]
    own_tiles = peak_ref.shape[0]
    row_tiles = grad_ref.shape[0] - 1
    slots = found_ref.shape[0] - group_size
    active = lax.axis_index("cell") % 2 == parity

    @pl.when(active)
    def _():
        groups = spread(found_ref, index, stratum, counts[0, stratum], part, own_tiles, peak_tiles, slots)
        peak_grad[...] = jnp.zeros_like(peak_grad)
        grad_ref[...] = jnp.zeros_like(grad_ref) if fresh else given[...]
        slot_of = lambda k: slot_at(found_ref, k, slots, row_tiles, own_tiles, peak_tiles)
        walk(groups, slot_of, cell_ref, peak_ref, lambda t: values[0, t], peak_grad, grad_ref, scaling)
        for c in range(own_tiles):
            new_ref[c] = stepped(peak_ref[c], peak_grad[c], scaling)

    if closing:
        near = out_ref.shape[0]

        def close(source):
            for r in range(row_tiles):
                total = source[r]
                for one in earlier:
                    total = total + one[r]
                out_ref[r % near, r // near] = (total * (gradient_scale * scaling)).astype(out_ref.dtype)

        @pl.when(active)
        def _():
            close(grad_ref)

        @pl.when(jnp.logical_not(active))
        def _():
            close(other)


def place_kernel(part, even_ref, odd_ref, *refs):
    out_ref, sem = refs[-2:]
    own_tiles = even_ref.shape[0]
    odd = lax.axis_index("cell") % 2
    for parity, piece_ref in enumerate((even_ref, odd_ref)):

        @pl.when(odd == parity)
        def _():
            copy = pltpu.make_async_copy(piece_ref, out_ref.at[pl.ds(part * own_tiles, own_tiles)], sem)
            copy.start()
            copy.wait()


def cost(flops, read):
    return pl.CostEstimate(flops=flops, bytes_accessed=read, transcendentals=0)


def per_device(cell_factors, peak_factors, tile_values, tile_index, tile_counts):
    cell_dev, rank_width = cell_factors.shape
    strata, slots, tile_size, _ = tile_values.shape
    block_rows = peak_factors.shape[0]
    row_tiles = cell_dev // tile_size
    peak_tiles = block_rows // tile_size
    own_tiles = peak_tiles // parts
    chroms = lax.axis_size("chrom")
    cells = lax.axis_size("cell")
    share_rows = cell_dev // chroms
    assert share_rows == tile_size and strata == 3 and cells % 2 == 0
    near = chroms // 2
    scaling = 1.0 / math.sqrt(rank_width)
    flops = 6 * slots * tile_size * tile_size * rank_width // parts
    cell_blocks = cell_factors.reshape(row_tiles, tile_size, rank_width)
    peak_block = peak_factors.reshape(peak_tiles, tile_size, rank_width)
    counts = tile_counts.T
    even, odd = 0, 1

    swap = [(i, i ^ 1) for i in range(cells)]
    down = [(i, (i - 1) % cells) for i in range(cells)]
    up = [[(i, (i + 2) % cells if i % 2 == parity else i) for i in range(cells)] for parity in (even, odd)]
    moved = lambda piece, pairs: lax.ppermute(piece, "cell", pairs)

    piece_out = jax.ShapeDtypeStruct((own_tiles, tile_size, rank_width), jnp.bfloat16)
    grad_out = jax.ShapeDtypeStruct((row_tiles + 1, tile_size, rank_width), jnp.float32)
    token_out = jax.ShapeDtypeStruct((8, lanes), jnp.int32)
    step_scratch = [
        pltpu.VMEM((own_tiles + 1, tile_size, rank_width), jnp.float32),
        pltpu.SMEM((slots + group_size,), jnp.int32),
    ]

    def first_call(part, before):
        return pl.pallas_call(
            functools.partial(first_kernel, scaling, part, peak_tiles),
            grid=(1,),
            out_shape=(piece_out, grad_out),
            in_specs=[smem, smem, far, far, far] + [far] * len(before),
            out_specs=(vmem, vmem),
            scratch_shapes=[
                pltpu.VMEM(cell_blocks.shape, jnp.bfloat16),
                pltpu.VMEM(piece_out.shape, jnp.bfloat16),
                pltpu.VMEM(tile_values.shape[1:], jnp.bfloat16),
                *step_scratch,
                pltpu.SemaphoreType.DMA((3,)),
            ],
            compiler_params=pltpu.CompilerParams(vmem_limit_bytes=60 * mebi),
            cost_estimate=cost(flops, 3 * mebi),
        )(counts, tile_index, cell_blocks, peak_block, tile_values, *before)

    def part_call(stratum, part, parity, piece, given, token, closing=None):
        weight = 16 if (stratum, parity) == (2, odd) else 0
        own_values = pl.BlockSpec((1,) + tile_values.shape[1:], lambda i: (stratum, 0, 0, 0))
        args = [counts, tile_index, cell_blocks, tile_values, piece]
        in_specs = [smem, smem, vmem, own_values, vmem]
        if given is not None:
            args.append(given)
            in_specs.append(vmem)
        args.append(token)
        in_specs.append(far)
        if closing is None:
            out_shape, out_specs, scratch = (piece_out, grad_out, token_out), (vmem, vmem, far), step_scratch
        else:
            args += closing
            in_specs += [vmem] * len(closing)
            sums = jax.ShapeDtypeStruct((near, chroms // near, share_rows, rank_width), jnp.bfloat16)
            out_shape, out_specs = (piece_out, sums), (vmem, vmem)
            scratch = [pltpu.VMEM(grad_out.shape, jnp.float32), *step_scratch]
        return pl.pallas_call(
            functools.partial(part_kernel, scaling, stratum, part, parity, peak_tiles, closing is not None, given is None),
            grid=(1,),
            out_shape=out_shape,
            in_specs=in_specs,
            out_specs=out_specs,
            scratch_shapes=scratch,
            compiler_params=pltpu.CompilerParams(vmem_limit_bytes=16 * mebi),
            cost_estimate=cost(0, weight * mebi),
        )(*args)

    halves = range(parts)
    near_in, far_in, earlier = [], [], []
    for part in halves:
        piece, grad = first_call(part, earlier)
        near_in.append(moved(piece, swap))
        far_in.append(moved(piece, down))
        earlier.append(grad)
    token = earlier[-1]
    even_grad = odd_grad = None
    sent_down, swapped, ends = [], [], [[], []]
    for part in halves:
        piece, even_grad, token = part_call(1, part, even, near_in[part], even_grad, token)
        sent_down.append(moved(piece, down))
    for part in halves:
        piece, odd_grad, token = part_call(1, part, odd, far_in[part], odd_grad, token)
        swapped.append(moved(piece, swap))
    for part in halves:
        piece, odd_grad, token = part_call(2, part, odd, sent_down[part], odd_grad, token)
        ends[odd].append(moved(piece, up[odd]))
    for part in halves:
        if part < parts - 1:
            piece, even_grad, token = part_call(2, part, even, swapped[part], even_grad, token)
        else:
            piece, grad = part_call(2, part, even, swapped[part], even_grad, token, earlier + [odd_grad])
        ends[even].append(moved(piece, up[even]))

    def put(part, peak_out):
        args = [ends[even][part], ends[odd][part]] + ([] if peak_out is None else [peak_out])
        return pl.pallas_call(
            functools.partial(place_kernel, part),
            grid=(1,),
            out_shape=jax.ShapeDtypeStruct(peak_block.shape, jnp.bfloat16),
            in_specs=[vmem, vmem, far][: len(args)],
            out_specs=far,
            scratch_shapes=[pltpu.SemaphoreType.DMA],
            input_output_aliases={} if peak_out is None else {2: 0},
            compiler_params=pltpu.CompilerParams(vmem_limit_bytes=16 * mebi),
            cost_estimate=cost(0, 8 * mebi),
        )(*args)

    rings = [list(range(r * near, (r + 1) * near)) for r in range(chroms // near)]
    shares = lax.all_to_all(grad, "chrom", 0, 0, axis_index_groups=rings, tiled=True)
    peak_out = None
    for part in range(parts - 1):
        peak_out = put(part, peak_out)
    peak_out, shares = lax.optimization_barrier((peak_out, shares))
    shares = jnp.sum(shares.astype(jnp.float32), axis=0)
    side = lax.axis_index("chrom") // near
    kept = lax.dynamic_index_in_dim(shares, side, 0, keepdims=False)
    sent = lax.dynamic_index_in_dim(shares, 1 - side, 0, keepdims=False).astype(jnp.bfloat16)
    got = lax.ppermute(sent, "chrom", [(j, (j + near) % chroms) for j in range(chroms)])
    peak_out = put(parts - 1, peak_out)
    peak_out, got = lax.optimization_barrier((peak_out, got))
    summed = kept + got.astype(jnp.float32)
    return (peak_out.reshape(block_rows, rank_width), summed)


def solution(mesh):
    in_specs = (
        P("cell", None),
        P(("cell", "chrom"), None),
        P("cell", "chrom", None, None),
        P("cell", "chrom"),
        P("cell", "chrom"),
    )
    out_specs = (P(("cell", "chrom"), None), P(("cell", "chrom"), None))
    return jax.shard_map(
        per_device, mesh=mesh, in_specs=in_specs, out_specs=out_specs, check_vma=False
    )
```

```python
import functools
import math

import jax
import jax.numpy as jnp
from jax import lax
from jax.experimental import pallas as pl
from jax.experimental.pallas import tpu as pltpu
from jax.sharding import PartitionSpec as P

learning_rate = 0.15
gradient_scale = 0.1
parts = 2
group_size = 8
lanes = 128
mebi = 1024 * 1024

smem = pl.BlockSpec(memory_space=pltpu.SMEM)
vmem = pl.BlockSpec(memory_space=pltpu.VMEM)
far = pl.BlockSpec(memory_space=pltpu.HBM)


def contract(left, right, dims):
    return lax.dot_general(left, right, ((dims[:1], dims[1:]), ((), ())), preferred_element_type=jnp.float32)


def walk(groups, slot_of, cell_ref, peak_ref, values_at, peak_grad, grad_ref, scaling):
    def tiles(start, count):
        found = [slot_of(start + k) for k in range(count)]
        resids = []
        for t, row, col, _, _ in found:
            predicted = contract(cell_ref[row], peak_ref[col], (1, 1))
            resids.append((predicted * scaling - values_at(t).astype(jnp.float32)).astype(jnp.bfloat16))
        terms = [contract(r, cell_ref[f[1]], (0, 0)) for r, f in zip(resids, found)]
        for term, f in zip(terms, found):
            peak_grad[f[4]] += term
        terms = [contract(r, peak_ref[f[2]], (1, 0)) for r, f in zip(resids, found)]
        for term, f in zip(terms, found):
            grad_ref[f[3]] += term

    pairs = groups // 2

    def pair(g, carry):
        tiles(g * 2 * group_size, 2 * group_size)
        return carry

    lax.fori_loop(0, pairs, pair, 0)

    @pl.when(groups > 2 * pairs)
    def _():
        tiles(pairs * 2 * group_size, group_size)


def stepped(peak, grad, scaling):
    return (peak.astype(jnp.float32) - learning_rate * (grad * scaling)).astype(jnp.bfloat16)


def first_kernel(scaling, counts, index, cell_in, peak_in, values_in, *refs):
    news, (grad_ref, cell_ref, peak_ref, values_ref, peak_grad, sems) = refs[:parts], refs[parts:]
    peak_tiles = peak_ref.shape[0]
    loads = [
        pltpu.make_async_copy(cell_in, cell_ref, sems.at[0]),
        pltpu.make_async_copy(peak_in, peak_ref, sems.at[1]),
        pltpu.make_async_copy(values_in.at[0], values_ref, sems.at[2]),
    ]
    for copy in loads:
        copy.start()
    peak_grad[...] = jnp.zeros_like(peak_grad)
    grad_ref[...] = jnp.zeros_like(grad_ref)
    for copy in loads:
        copy.wait()

    def slot_of(t):
        place = index[0, t]
        row, col = place // peak_tiles, place % peak_tiles
        return t, row, col, row, col

    groups = counts[0, 0] // group_size
    walk(groups, slot_of, cell_ref, peak_ref, lambda t: values_ref[t], peak_grad, grad_ref, scaling)
    own_tiles = peak_tiles // parts
    for c in range(peak_tiles):
        news[c // own_tiles][c % own_tiles] = stepped(peak_ref[c], peak_grad[c], scaling)


def part_kernel(scaling, stratum, part, peak_tiles, closing, fresh, *refs):
    counts, index, cell_ref, values, peak_ref, *rest = refs
    given = None
    if not fresh:
        given, *rest = rest
    if closing:
        early, new_ref, out_ref, grad_ref, peak_grad, places = rest
    else:
        new_ref, grad_ref, peak_grad, places = rest
    own_tiles = peak_ref.shape[0]
    row_tiles = grad_ref.shape[0] - 1
    slots = places.shape[0] - group_size

    def note(t, found):
        place = index[stratum, t]
        places[found] = place * slots + t
        mine = (place % peak_tiles) // own_tiles == part
        return found + jnp.where(mine, 1, 0)

    found = lax.fori_loop(0, counts[0, stratum], note, 0)
    for k in range(group_size):
        places[found + k] = -1
    peak_grad[...] = jnp.zeros_like(peak_grad)
    grad_ref[...] = jnp.zeros_like(grad_ref) if fresh else given[...]

    def slot_of(k):
        code = places[k]
        used = code >= 0
        code = jnp.maximum(code, 0)
        place = code // slots
        row, col = place // peak_tiles, place % own_tiles
        return code % slots, row, col, jnp.where(used, row, row_tiles), jnp.where(used, col, own_tiles)

    groups = (found + group_size - 1) // group_size
    walk(groups, slot_of, cell_ref, peak_ref, lambda t: values[0, t], peak_grad, grad_ref, scaling)
    for c in range(own_tiles):
        new_ref[c] = stepped(peak_ref[c], peak_grad[c], scaling)
    if closing:
        near = out_ref.shape[0]
        for r in range(row_tiles):
            out_ref[r % near, r // near] = ((early[r] + grad_ref[r]) * (gradient_scale * scaling)).astype(out_ref.dtype)


def place_kernel(part, piece_ref, *refs):
    out_ref, sem = refs[-2:]
    own_tiles = piece_ref.shape[0]
    copy = pltpu.make_async_copy(piece_ref, out_ref.at[pl.ds(part * own_tiles, own_tiles)], sem)
    copy.start()
    copy.wait()


def cost(flops, read):
    return pl.CostEstimate(flops=flops, bytes_accessed=read, transcendentals=0)


def per_device(cell_factors, peak_factors, tile_values, tile_index, tile_counts):
    cell_dev, rank_width = cell_factors.shape
    strata, slots, tile_size, _ = tile_values.shape
    block_rows = peak_factors.shape[0]
    row_tiles = cell_dev // tile_size
    peak_tiles = block_rows // tile_size
    own_tiles = peak_tiles // parts
    chroms = lax.axis_size("chrom")
    cells = lax.axis_size("cell")
    share_rows = cell_dev // chroms
    assert share_rows == tile_size
    near = chroms // 2
    scaling = 1.0 / math.sqrt(rank_width)
    flops = 6 * slots * tile_size * tile_size * rank_width
    cell_blocks = cell_factors.reshape(row_tiles, tile_size, rank_width)
    peak_block = peak_factors.reshape(peak_tiles, tile_size, rank_width)
    counts = tile_counts.T
    last = strata - 1

    def moved(piece, by):
        return lax.ppermute(piece, "cell", [(i, (i + by) % cells) for i in range(cells)])

    piece_out = jax.ShapeDtypeStruct((own_tiles, tile_size, rank_width), jnp.bfloat16)
    grad_out = jax.ShapeDtypeStruct((row_tiles + 1, tile_size, rank_width), jnp.float32)

    *pieces, early = pl.pallas_call(
        functools.partial(first_kernel, scaling),
        grid=(1,),
        out_shape=(piece_out,) * parts + (jax.ShapeDtypeStruct(cell_blocks.shape, jnp.float32),),
        in_specs=[smem, smem, far, far, far],
        out_specs=(vmem,) * (parts + 1),
        scratch_shapes=[
            pltpu.VMEM(cell_blocks.shape, jnp.bfloat16),
            pltpu.VMEM(peak_block.shape, jnp.bfloat16),
            pltpu.VMEM(tile_values.shape[1:], jnp.bfloat16),
            pltpu.VMEM(peak_block.shape, jnp.float32),
            pltpu.SemaphoreType.DMA((3,)),
        ],
        compiler_params=pltpu.CompilerParams(vmem_limit_bytes=60 * mebi),
        cost_estimate=cost(flops, 4 * mebi),
    )(counts, tile_index, cell_blocks, peak_block, tile_values)
    pieces = [moved(piece, -1) for piece in pieces]

    def part_call(stratum, part, piece, given, closing):
        own_values = pl.BlockSpec((1,) + tile_values.shape[1:], lambda i: (stratum, 0, 0, 0))
        args = [counts, tile_index, cell_blocks, tile_values, piece]
        in_specs = [smem, smem, vmem, own_values, vmem]
        if given is not None:
            args.append(given)
        if closing:
            args.append(early)
        in_specs += [vmem] * (len(args) - len(in_specs))
        scratch = [
            pltpu.VMEM((own_tiles + 1, tile_size, rank_width), jnp.float32),
            pltpu.SMEM((slots + group_size,), jnp.int32),
        ]
        second = grad_out
        if closing:
            second = jax.ShapeDtypeStruct((near, chroms // near, share_rows, rank_width), jnp.bfloat16)
            scratch.insert(0, pltpu.VMEM(grad_out.shape, jnp.float32))
        return pl.pallas_call(
            functools.partial(part_kernel, scaling, stratum, part, peak_tiles, closing, given is None),
            grid=(1,),
            out_shape=(piece_out, second),
            in_specs=in_specs,
            out_specs=(vmem, vmem),
            scratch_shapes=scratch,
            compiler_params=pltpu.CompilerParams(vmem_limit_bytes=16 * mebi),
            cost_estimate=cost(flops // parts, 3 * mebi),
        )(*args)

    grad = None
    for stratum in range(1, strata):
        for part in range(parts):
            closing = stratum == last and part == parts - 1
            piece, grad = part_call(stratum, part, pieces[part], grad, closing)
            pieces[part] = moved(piece, last if stratum == last else -1)

    def put(part, peak_out):
        args = [pieces[part]] + ([] if peak_out is None else [peak_out])
        return pl.pallas_call(
            functools.partial(place_kernel, part),
            grid=(1,),
            out_shape=jax.ShapeDtypeStruct(peak_block.shape, jnp.bfloat16),
            in_specs=[vmem, far][: len(args)],
            out_specs=far,
            scratch_shapes=[pltpu.SemaphoreType.DMA],
            input_output_aliases={} if peak_out is None else {1: 0},
            compiler_params=pltpu.CompilerParams(vmem_limit_bytes=16 * mebi),
            cost_estimate=cost(0, 8 * mebi),
        )(*args)

    rings = [list(range(r * near, (r + 1) * near)) for r in range(chroms // near)]
    shares = lax.all_to_all(grad, "chrom", 0, 0, axis_index_groups=rings, tiled=True)
    peak_out = None
    for part in range(parts - 1):
        peak_out = put(part, peak_out)
    peak_out, shares = lax.optimization_barrier((peak_out, shares))
    shares = jnp.sum(shares.astype(jnp.float32), axis=0)
    side = lax.axis_index("chrom") // near
    kept = lax.dynamic_index_in_dim(shares, side, 0, keepdims=False)
    sent = lax.dynamic_index_in_dim(shares, 1 - side, 0, keepdims=False).astype(jnp.bfloat16)
    got = lax.ppermute(sent, "chrom", [(j, (j + near) % chroms) for j in range(chroms)])
    summed = kept + got.astype(jnp.float32)
    summed, pieces[-1] = lax.optimization_barrier((summed, pieces[-1]))
    peak_out = put(parts - 1, peak_out)
    return (peak_out.reshape(block_rows, rank_width), summed)


def solution(mesh):
    in_specs = (
        P("cell", None),
        P(("cell", "chrom"), None),
        P("cell", "chrom", None, None),
        P("cell", "chrom"),
        P("cell", "chrom"),
    )
    out_specs = (P(("cell", "chrom"), None), P(("cell", "chrom"), None))
    return jax.shard_map(
        per_device, mesh=mesh, in_specs=in_specs, out_specs=out_specs, check_vma=False
    )
```

```python
import functools
import math

import jax
import jax.numpy as jnp
from jax import lax
from jax.experimental import pallas as pl
from jax.experimental.pallas import tpu as pltpu
from jax.sharding import PartitionSpec as P

learning_rate = 0.15
gradient_scale = 0.1
parts = 2
group_size = 8
lanes = 128
mebi = 1024 * 1024

smem = pl.BlockSpec(memory_space=pltpu.SMEM)
vmem = pl.BlockSpec(memory_space=pltpu.VMEM)
far = pl.BlockSpec(memory_space=pltpu.HBM)


def contract(left, right, dims):
    return lax.dot_general(left, right, ((dims[:1], dims[1:]), ((), ())), preferred_element_type=jnp.float32)


def walk(groups, slot_of, cell_ref, peak_ref, values_at, peak_grad, grad_ref, scaling):
    def tiles(start, count):
        found = [slot_of(start + k) for k in range(count)]
        resids = []
        for t, row, col, _, _ in found:
            predicted = contract(cell_ref[row], peak_ref[col], (1, 1))
            resids.append((predicted * scaling - values_at(t).astype(jnp.float32)).astype(jnp.bfloat16))
        if peak_grad is not None:
            terms = [contract(r, cell_ref[f[1]], (0, 0)) for r, f in zip(resids, found)]
            for term, f in zip(terms, found):
                peak_grad[f[4]] += term
        if grad_ref is not None:
            terms = [contract(r, peak_ref[f[2]], (1, 0)) for r, f in zip(resids, found)]
            for term, f in zip(terms, found):
                grad_ref[f[3]] += term

    pairs = groups // 2

    def pair(g, carry):
        tiles(g * 2 * group_size, 2 * group_size)
        return carry

    lax.fori_loop(0, pairs, pair, 0)

    @pl.when(groups > 2 * pairs)
    def _():
        tiles(pairs * 2 * group_size, group_size)


def stepped(peak, grad, scaling):
    return (peak.astype(jnp.float32) - learning_rate * (grad * scaling)).astype(jnp.bfloat16)


def first_kernel(scaling, counts, index, cell_in, peak_in, values_in, *refs):
    news, (cell_ref, peak_ref, values_ref, peak_grad, sems) = refs[:parts], refs[parts:]
    peak_tiles = peak_ref.shape[0]
    loads = [
        pltpu.make_async_copy(cell_in, cell_ref, sems.at[0]),
        pltpu.make_async_copy(peak_in, peak_ref, sems.at[1]),
        pltpu.make_async_copy(values_in.at[0], values_ref, sems.at[2]),
    ]
    for copy in loads:
        copy.start()
    peak_grad[...] = jnp.zeros_like(peak_grad)
    for copy in loads:
        copy.wait()

    def slot_of(t):
        place = index[0, t]
        row, col = place // peak_tiles, place % peak_tiles
        return t, row, col, row, col

    groups = counts[0, 0] // group_size
    walk(groups, slot_of, cell_ref, peak_ref, lambda t: values_ref[t], peak_grad, None, scaling)
    own_tiles = peak_tiles // parts
    for c in range(peak_tiles):
        news[c // own_tiles][c % own_tiles] = stepped(peak_ref[c], peak_grad[c], scaling)


def cell_kernel(scaling, counts, index, cell_ref, peak_ref, values, grad_ref):
    peak_tiles = peak_ref.shape[0]
    grad_ref[...] = jnp.zeros_like(grad_ref)

    def slot_of(t):
        place = index[0, t]
        row, col = place // peak_tiles, place % peak_tiles
        return t, row, col, row, col

    groups = counts[0, 0] // group_size
    walk(groups, slot_of, cell_ref, peak_ref, lambda t: values[0, t], None, grad_ref, scaling)


def part_kernel(scaling, stratum, part, peak_tiles, closing, fresh, *refs):
    counts, index, cell_ref, values, peak_ref, *rest = refs
    given = None
    if not fresh:
        given, *rest = rest
    if closing:
        new_ref, out_ref, grad_ref, peak_grad, places = rest
    else:
        new_ref, grad_ref, peak_grad, places = rest
    own_tiles = peak_ref.shape[0]
    row_tiles = grad_ref.shape[0] - 1
    slots = places.shape[0] - group_size

    def note(t, found):
        place = index[stratum, t]
        places[found] = place * slots + t
        mine = (place % peak_tiles) // own_tiles == part
        return found + jnp.where(mine, 1, 0)

    found = lax.fori_loop(0, counts[0, stratum], note, 0)
    for k in range(group_size):
        places[found + k] = -1
    peak_grad[...] = jnp.zeros_like(peak_grad)
    grad_ref[...] = jnp.zeros_like(grad_ref) if fresh else given[...]

    def slot_of(k):
        code = places[k]
        used = code >= 0
        code = jnp.maximum(code, 0)
        place = code // slots
        row, col = place // peak_tiles, place % own_tiles
        return code % slots, row, col, jnp.where(used, row, row_tiles), jnp.where(used, col, own_tiles)

    groups = (found + group_size - 1) // group_size
    walk(groups, slot_of, cell_ref, peak_ref, lambda t: values[0, t], peak_grad, grad_ref, scaling)
    for c in range(own_tiles):
        new_ref[c] = stepped(peak_ref[c], peak_grad[c], scaling)
    if closing:
        near = out_ref.shape[0]
        for r in range(row_tiles):
            out_ref[r % near, r // near] = (grad_ref[r] * (gradient_scale * scaling)).astype(out_ref.dtype)


def place_kernel(part, piece_ref, *refs):
    out_ref, sem = refs[-2:]
    own_tiles = piece_ref.shape[0]
    copy = pltpu.make_async_copy(piece_ref, out_ref.at[pl.ds(part * own_tiles, own_tiles)], sem)
    copy.start()
    copy.wait()


def cost(flops, read):
    return pl.CostEstimate(flops=flops, bytes_accessed=read, transcendentals=0)


def per_device(cell_factors, peak_factors, tile_values, tile_index, tile_counts):
    cell_dev, rank_width = cell_factors.shape
    strata, slots, tile_size, _ = tile_values.shape
    block_rows = peak_factors.shape[0]
    row_tiles = cell_dev // tile_size
    peak_tiles = block_rows // tile_size
    own_tiles = peak_tiles // parts
    chroms = lax.axis_size("chrom")
    cells = lax.axis_size("cell")
    share_rows = cell_dev // chroms
    assert share_rows == tile_size
    near = chroms // 2
    scaling = 1.0 / math.sqrt(rank_width)
    flops = 6 * slots * tile_size * tile_size * rank_width
    cell_blocks = cell_factors.reshape(row_tiles, tile_size, rank_width)
    peak_block = peak_factors.reshape(peak_tiles, tile_size, rank_width)
    counts = tile_counts.T
    last = strata - 1

    def moved(piece, by):
        return lax.ppermute(piece, "cell", [(i, (i + by) % cells) for i in range(cells)])

    piece_out = jax.ShapeDtypeStruct((own_tiles, tile_size, rank_width), jnp.bfloat16)
    grad_out = jax.ShapeDtypeStruct((row_tiles + 1, tile_size, rank_width), jnp.float32)

    pieces = pl.pallas_call(
        functools.partial(first_kernel, scaling),
        grid=(1,),
        out_shape=(piece_out,) * parts,
        in_specs=[smem, smem, far, far, far],
        out_specs=(vmem,) * parts,
        scratch_shapes=[
            pltpu.VMEM(cell_blocks.shape, jnp.bfloat16),
            pltpu.VMEM(peak_block.shape, jnp.bfloat16),
            pltpu.VMEM(tile_values.shape[1:], jnp.bfloat16),
            pltpu.VMEM(peak_block.shape, jnp.float32),
            pltpu.SemaphoreType.DMA((3,)),
        ],
        compiler_params=pltpu.CompilerParams(vmem_limit_bytes=60 * mebi),
        cost_estimate=cost(flops, 4 * mebi),
    )(counts, tile_index, cell_blocks, peak_block, tile_values)
    pieces = [moved(piece, -1) for piece in pieces]
    first_values = pl.BlockSpec((1,) + tile_values.shape[1:], lambda i: (0, 0, 0, 0))
    grad = pl.pallas_call(
        functools.partial(cell_kernel, scaling),
        grid=(1,),
        out_shape=grad_out,
        in_specs=[smem, smem, vmem, vmem, first_values],
        out_specs=vmem,
        compiler_params=pltpu.CompilerParams(vmem_limit_bytes=16 * mebi),
        cost_estimate=cost(flops, 4 * mebi),
    )(counts, tile_index, cell_blocks, peak_block, tile_values)

    def part_call(stratum, part, piece, given, closing):
        own_values = pl.BlockSpec((1,) + tile_values.shape[1:], lambda i: (stratum, 0, 0, 0))
        args = [counts, tile_index, cell_blocks, tile_values, piece]
        in_specs = [smem, smem, vmem, own_values, vmem]
        if given is not None:
            args.append(given)
        in_specs += [vmem] * (len(args) - len(in_specs))
        scratch = [
            pltpu.VMEM((own_tiles + 1, tile_size, rank_width), jnp.float32),
            pltpu.SMEM((slots + group_size,), jnp.int32),
        ]
        second = grad_out
        if closing:
            second = jax.ShapeDtypeStruct((near, chroms // near, share_rows, rank_width), jnp.bfloat16)
            scratch.insert(0, pltpu.VMEM(grad_out.shape, jnp.float32))
        return pl.pallas_call(
            functools.partial(part_kernel, scaling, stratum, part, peak_tiles, closing, given is None),
            grid=(1,),
            out_shape=(piece_out, second),
            in_specs=in_specs,
            out_specs=(vmem, vmem),
            scratch_shapes=scratch,
            compiler_params=pltpu.CompilerParams(vmem_limit_bytes=16 * mebi),
            cost_estimate=cost(flops // parts, 3 * mebi),
        )(*args)

    for stratum in range(1, strata):
        for part in range(parts):
            closing = stratum == last and part == parts - 1
            piece, grad = part_call(stratum, part, pieces[part], grad, closing)
            pieces[part] = moved(piece, last if stratum == last else -1)

    def put(part, peak_out):
        args = [pieces[part]] + ([] if peak_out is None else [peak_out])
        return pl.pallas_call(
            functools.partial(place_kernel, part),
            grid=(1,),
            out_shape=jax.ShapeDtypeStruct(peak_block.shape, jnp.bfloat16),
            in_specs=[vmem, far][: len(args)],
            out_specs=far,
            scratch_shapes=[pltpu.SemaphoreType.DMA],
            input_output_aliases={} if peak_out is None else {1: 0},
            compiler_params=pltpu.CompilerParams(vmem_limit_bytes=16 * mebi),
            cost_estimate=cost(0, 8 * mebi),
        )(*args)

    rings = [list(range(r * near, (r + 1) * near)) for r in range(chroms // near)]
    shares = lax.all_to_all(grad, "chrom", 0, 0, axis_index_groups=rings, tiled=True)
    peak_out = None
    for part in range(parts - 1):
        peak_out = put(part, peak_out)
    peak_out, shares = lax.optimization_barrier((peak_out, shares))
    shares = jnp.sum(shares.astype(jnp.float32), axis=0)
    side = lax.axis_index("chrom") // near
    kept = lax.dynamic_index_in_dim(shares, side, 0, keepdims=False)
    sent = lax.dynamic_index_in_dim(shares, 1 - side, 0, keepdims=False).astype(jnp.bfloat16)
    got = lax.ppermute(sent, "chrom", [(j, (j + near) % chroms) for j in range(chroms)])
    summed = kept + got.astype(jnp.float32)
    summed, pieces[-1] = lax.optimization_barrier((summed, pieces[-1]))
    peak_out = put(parts - 1, peak_out)
    return (peak_out.reshape(block_rows, rank_width), summed)


def solution(mesh):
    in_specs = (
        P("cell", None),
        P(("cell", "chrom"), None),
        P("cell", "chrom", None, None),
        P("cell", "chrom"),
        P("cell", "chrom"),
    )
    out_specs = (P(("cell", "chrom"), None), P(("cell", "chrom"), None))
    return jax.shard_map(
        per_device, mesh=mesh, in_specs=in_specs, out_specs=out_specs, check_vma=False
    )
```

```python
import functools
import math

import jax
import jax.numpy as jnp
from jax import lax
from jax.experimental import pallas as pl
from jax.experimental.pallas import tpu as pltpu
from jax.sharding import PartitionSpec as P

learning_rate = 0.15
gradient_scale = 0.1
parts = 2
group_size = 8
lanes = 128
mebi = 1024 * 1024

smem = pl.BlockSpec(memory_space=pltpu.SMEM)
vmem = pl.BlockSpec(memory_space=pltpu.VMEM)
far = pl.BlockSpec(memory_space=pltpu.HBM)


def contract(left, right, dims):
    return lax.dot_general(left, right, ((dims[:1], dims[1:]), ((), ())), preferred_element_type=jnp.float32)


def walk(groups, slot_of, cell_ref, peak_ref, values_at, peak_grad, grad_ref, scaling):
    def tiles(start, count):
        found = [slot_of(start + k) for k in range(count)]
        resids = []
        for t, row, col, _, _ in found:
            predicted = contract(cell_ref[row], peak_ref[col], (1, 1))
            resids.append((predicted * scaling - values_at(t).astype(jnp.float32)).astype(jnp.bfloat16))
        if peak_grad is not None:
            terms = [contract(r, cell_ref[f[1]], (0, 0)) for r, f in zip(resids, found)]
            for term, f in zip(terms, found):
                peak_grad[f[4]] += term
        if grad_ref is not None:
            terms = [contract(r, peak_ref[f[2]], (1, 0)) for r, f in zip(resids, found)]
            for term, f in zip(terms, found):
                grad_ref[f[3]] += term

    pairs = groups // 2

    def pair(g, carry):
        tiles(g * 2 * group_size, 2 * group_size)
        return carry

    lax.fori_loop(0, pairs, pair, 0)

    @pl.when(groups > 2 * pairs)
    def _():
        tiles(pairs * 2 * group_size, group_size)


def stepped(peak, grad, scaling):
    return (peak.astype(jnp.float32) - learning_rate * (grad * scaling)).astype(jnp.bfloat16)


def first_kernel(scaling, counts, index, cell_in, peak_in, values_in, *refs):
    news, (cell_ref, peak_ref, values_ref, peak_grad, sems) = refs[:parts], refs[parts:]
    peak_tiles = peak_ref.shape[0]
    loads = [
        pltpu.make_async_copy(cell_in, cell_ref, sems.at[0]),
        pltpu.make_async_copy(peak_in, peak_ref, sems.at[1]),
        pltpu.make_async_copy(values_in.at[0], values_ref, sems.at[2]),
    ]
    for copy in loads:
        copy.start()
    peak_grad[...] = jnp.zeros_like(peak_grad)
    for copy in loads:
        copy.wait()

    def slot_of(t):
        place = index[0, t]
        row, col = place // peak_tiles, place % peak_tiles
        return t, row, col, row, col

    groups = counts[0, 0] // group_size
    walk(groups, slot_of, cell_ref, peak_ref, lambda t: values_ref[t], peak_grad, None, scaling)
    own_tiles = peak_tiles // parts
    for c in range(peak_tiles):
        news[c // own_tiles][c % own_tiles] = stepped(peak_ref[c], peak_grad[c], scaling)


def cell_kernel(scaling, counts, index, cell_ref, peak_ref, values, grad_ref):
    peak_tiles = peak_ref.shape[0]
    grad_ref[...] = jnp.zeros_like(grad_ref)

    def slot_of(t):
        place = index[0, t]
        row, col = place // peak_tiles, place % peak_tiles
        return t, row, col, row, col

    groups = counts[0, 0] // group_size
    walk(groups, slot_of, cell_ref, peak_ref, lambda t: values[0, t], None, grad_ref, scaling)


def part_kernel(scaling, stratum, part, peak_tiles, closing, fresh, *refs):
    counts, index, cell_ref, values, peak_ref, *rest = refs
    given = None
    if not fresh:
        given, *rest = rest
    if closing:
        new_ref, *out_refs, grad_ref, peak_grad, places = rest
    else:
        new_ref, grad_ref, peak_grad, places = rest
    own_tiles = peak_ref.shape[0]
    row_tiles = grad_ref.shape[0] - 1
    slots = places.shape[0] - group_size

    def note(t, found):
        place = index[stratum, t]
        places[found] = place * slots + t
        mine = (place % peak_tiles) // own_tiles == part
        return found + jnp.where(mine, 1, 0)

    found = lax.fori_loop(0, counts[0, stratum], note, 0)
    for k in range(group_size):
        places[found + k] = -1
    peak_grad[...] = jnp.zeros_like(peak_grad)
    grad_ref[...] = jnp.zeros_like(grad_ref) if fresh else given[...]

    def slot_of(k):
        code = places[k]
        used = code >= 0
        code = jnp.maximum(code, 0)
        place = code // slots
        row, col = place // peak_tiles, place % own_tiles
        return code % slots, row, col, jnp.where(used, row, row_tiles), jnp.where(used, col, own_tiles)

    groups = (found + group_size - 1) // group_size
    walk(groups, slot_of, cell_ref, peak_ref, lambda t: values[0, t], peak_grad, grad_ref, scaling)
    for c in range(own_tiles):
        new_ref[c] = stepped(peak_ref[c], peak_grad[c], scaling)
    if closing:
        near = len(out_refs)
        spot = lax.axis_index("chrom") % near
        for ahead in range(near):
            for side in range(row_tiles // near):
                row = (spot + ahead) % near + side * near
                total = grad_ref[row] * (gradient_scale * scaling)
                out_refs[ahead][side] = total.astype(out_refs[ahead].dtype)


def place_kernel(part, piece_ref, *refs):
    out_ref, sem = refs[-2:]
    own_tiles = piece_ref.shape[0]
    copy = pltpu.make_async_copy(piece_ref, out_ref.at[pl.ds(part * own_tiles, own_tiles)], sem)
    copy.start()
    copy.wait()


def cost(flops, read):
    return pl.CostEstimate(flops=flops, bytes_accessed=read, transcendentals=0)


def per_device(cell_factors, peak_factors, tile_values, tile_index, tile_counts):
    cell_dev, rank_width = cell_factors.shape
    strata, slots, tile_size, _ = tile_values.shape
    block_rows = peak_factors.shape[0]
    row_tiles = cell_dev // tile_size
    peak_tiles = block_rows // tile_size
    own_tiles = peak_tiles // parts
    chroms = lax.axis_size("chrom")
    cells = lax.axis_size("cell")
    share_rows = cell_dev // chroms
    assert share_rows == tile_size
    near = chroms // 2
    scaling = 1.0 / math.sqrt(rank_width)
    flops = 6 * slots * tile_size * tile_size * rank_width
    cell_blocks = cell_factors.reshape(row_tiles, tile_size, rank_width)
    peak_block = peak_factors.reshape(peak_tiles, tile_size, rank_width)
    counts = tile_counts.T
    last = strata - 1

    def moved(piece, by):
        return lax.ppermute(piece, "cell", [(i, (i + by) % cells) for i in range(cells)])

    piece_out = jax.ShapeDtypeStruct((own_tiles, tile_size, rank_width), jnp.bfloat16)
    grad_out = jax.ShapeDtypeStruct((row_tiles + 1, tile_size, rank_width), jnp.float32)

    pieces = pl.pallas_call(
        functools.partial(first_kernel, scaling),
        grid=(1,),
        out_shape=(piece_out,) * parts,
        in_specs=[smem, smem, far, far, far],
        out_specs=(vmem,) * parts,
        scratch_shapes=[
            pltpu.VMEM(cell_blocks.shape, jnp.bfloat16),
            pltpu.VMEM(peak_block.shape, jnp.bfloat16),
            pltpu.VMEM(tile_values.shape[1:], jnp.bfloat16),
            pltpu.VMEM(peak_block.shape, jnp.float32),
            pltpu.SemaphoreType.DMA((3,)),
        ],
        compiler_params=pltpu.CompilerParams(vmem_limit_bytes=60 * mebi),
        cost_estimate=cost(flops, 4 * mebi),
    )(counts, tile_index, cell_blocks, peak_block, tile_values)
    pieces = [moved(piece, -1) for piece in pieces]
    first_values = pl.BlockSpec((1,) + tile_values.shape[1:], lambda i: (0, 0, 0, 0))
    grad = pl.pallas_call(
        functools.partial(cell_kernel, scaling),
        grid=(1,),
        out_shape=grad_out,
        in_specs=[smem, smem, vmem, vmem, first_values],
        out_specs=vmem,
        compiler_params=pltpu.CompilerParams(vmem_limit_bytes=16 * mebi),
        cost_estimate=cost(flops, 4 * mebi),
    )(counts, tile_index, cell_blocks, peak_block, tile_values)

    def part_call(stratum, part, piece, given, closing):
        own_values = pl.BlockSpec((1,) + tile_values.shape[1:], lambda i: (stratum, 0, 0, 0))
        args = [counts, tile_index, cell_blocks, tile_values, piece]
        in_specs = [smem, smem, vmem, own_values, vmem]
        if given is not None:
            args.append(given)
        in_specs += [vmem] * (len(args) - len(in_specs))
        scratch = [
            pltpu.VMEM((own_tiles + 1, tile_size, rank_width), jnp.float32),
            pltpu.SMEM((slots + group_size,), jnp.int32),
        ]
        others = (grad_out,)
        if closing:
            others = (jax.ShapeDtypeStruct((chroms // near, share_rows, rank_width), jnp.bfloat16),) * near
            scratch.insert(0, pltpu.VMEM(grad_out.shape, jnp.float32))
        return pl.pallas_call(
            functools.partial(part_kernel, scaling, stratum, part, peak_tiles, closing, given is None),
            grid=(1,),
            out_shape=(piece_out,) + others,
            in_specs=in_specs,
            out_specs=(vmem,) * (1 + len(others)),
            scratch_shapes=scratch,
            compiler_params=pltpu.CompilerParams(vmem_limit_bytes=16 * mebi),
            cost_estimate=cost(flops // parts, 3 * mebi),
        )(*args)

    for stratum in range(1, strata):
        for part in range(parts):
            closing = stratum == last and part == parts - 1
            piece, *grads = part_call(stratum, part, pieces[part], grad, closing)
            grad = grads[0]
            pieces[part] = moved(piece, last if stratum == last else -1)

    def put(part, peak_out):
        args = [pieces[part]] + ([] if peak_out is None else [peak_out])
        return pl.pallas_call(
            functools.partial(place_kernel, part),
            grid=(1,),
            out_shape=jax.ShapeDtypeStruct(peak_block.shape, jnp.bfloat16),
            in_specs=[vmem, far][: len(args)],
            out_specs=far,
            scratch_shapes=[pltpu.SemaphoreType.DMA],
            input_output_aliases={} if peak_out is None else {1: 0},
            compiler_params=pltpu.CompilerParams(vmem_limit_bytes=16 * mebi),
            cost_estimate=cost(0, 8 * mebi),
        )(*args)

    around = [j // near * near for j in range(chroms)]
    shares = grads[:1] + [
        lax.ppermute(grads[d], "chrom", [(j, around[j] + (j + d) % near) for j in range(chroms)])
        for d in range(1, near)
    ]
    peak_out = None
    for part in range(parts - 1):
        peak_out = put(part, peak_out)
    peak_out, shares = lax.optimization_barrier((peak_out, shares))
    shares = sum(share.astype(jnp.float32) for share in shares)
    side = lax.axis_index("chrom") // near
    kept = lax.dynamic_index_in_dim(shares, side, 0, keepdims=False)
    sent = lax.dynamic_index_in_dim(shares, 1 - side, 0, keepdims=False).astype(jnp.bfloat16)
    got = lax.ppermute(sent, "chrom", [(j, (j + near) % chroms) for j in range(chroms)])
    summed = kept + got.astype(jnp.float32)
    summed, pieces[-1] = lax.optimization_barrier((summed, pieces[-1]))
    peak_out = put(parts - 1, peak_out)
    return (peak_out.reshape(block_rows, rank_width), summed)


def solution(mesh):
    in_specs = (
        P("cell", None),
        P(("cell", "chrom"), None),
        P("cell", "chrom", None, None),
        P("cell", "chrom"),
        P("cell", "chrom"),
    )
    out_specs = (P(("cell", "chrom"), None), P(("cell", "chrom"), None))
    return jax.shard_map(
        per_device, mesh=mesh, in_specs=in_specs, out_specs=out_specs, check_vma=False
    )
```

```python
import functools
import math

import jax
import jax.numpy as jnp
from jax import lax
from jax.experimental import pallas as pl
from jax.experimental.pallas import tpu as pltpu
from jax.sharding import PartitionSpec as P

learning_rate = 0.15
gradient_scale = 0.1
parts = 2
group_size = 8
lanes = 128
mebi = 1024 * 1024

smem = pl.BlockSpec(memory_space=pltpu.SMEM)
vmem = pl.BlockSpec(memory_space=pltpu.VMEM)
far = pl.BlockSpec(memory_space=pltpu.HBM)


def contract(left, right, dims):
    return lax.dot_general(left, right, ((dims[:1], dims[1:]), ((), ())), preferred_element_type=jnp.float32)


def walk(groups, slot_of, cell_ref, peak_ref, values_at, peak_grad, grad_ref, scaling):
    def tiles(start, count):
        found = [slot_of(start + k) for k in range(count)]
        resids = []
        for t, row, col, _, _ in found:
            predicted = contract(cell_ref[row], peak_ref[col], (1, 1))
            resids.append((predicted * scaling - values_at(t).astype(jnp.float32)).astype(jnp.bfloat16))
        if peak_grad is not None:
            terms = [contract(r, cell_ref[f[1]], (0, 0)) for r, f in zip(resids, found)]
            for term, f in zip(terms, found):
                peak_grad[f[4]] += term
        if grad_ref is not None:
            terms = [contract(r, peak_ref[f[2]], (1, 0)) for r, f in zip(resids, found)]
            for term, f in zip(terms, found):
                grad_ref[f[3]] += term

    pairs = groups // 2

    def pair(g, carry):
        tiles(g * 2 * group_size, 2 * group_size)
        return carry

    lax.fori_loop(0, pairs, pair, 0)

    @pl.when(groups > 2 * pairs)
    def _():
        tiles(pairs * 2 * group_size, group_size)


def stepped(peak, grad, scaling):
    return (peak.astype(jnp.float32) - learning_rate * (grad * scaling)).astype(jnp.bfloat16)


def first_kernel(scaling, parity, counts, index, cell_in, peak_in, values_in, *refs):
    news, (grad_ref, cell_ref, peak_ref, values_ref, peak_grad, sems) = refs[-6 - parts : -6], refs[-6:]
    peak_tiles = peak_ref.shape[0]

    @pl.when(lax.axis_index("cell") % 2 == parity)
    def _():
        loads = [
            pltpu.make_async_copy(cell_in, cell_ref, sems.at[0]),
            pltpu.make_async_copy(peak_in, peak_ref, sems.at[1]),
            pltpu.make_async_copy(values_in.at[0], values_ref, sems.at[2]),
        ]
        for copy in loads:
            copy.start()
        peak_grad[...] = jnp.zeros_like(peak_grad)
        grad_ref[...] = jnp.zeros_like(grad_ref)
        for copy in loads:
            copy.wait()

        def slot_of(t):
            place = index[0, t]
            row, col = place // peak_tiles, place % peak_tiles
            return t, row, col, row, col

        groups = counts[0, 0] // group_size
        walk(groups, slot_of, cell_ref, peak_ref, lambda t: values_ref[t], peak_grad, grad_ref, scaling)
        own_tiles = peak_tiles // parts
        for c in range(peak_tiles):
            news[c // own_tiles][c % own_tiles] = stepped(peak_ref[c], peak_grad[c], scaling)


def part_kernel(scaling, stratum, part, peak_tiles, closing, paired, fresh, *refs):
    counts, index, cell_ref, values, peak_ref, *rest = refs
    if paired:
        far_ref, _, *rest, chosen = rest
        odd = lax.axis_index("cell") % 2

        @pl.when(odd == 0)
        def _():
            chosen[...] = peak_ref[...]

        @pl.when(odd == 1)
        def _():
            chosen[...] = far_ref[...]

        peak_ref = chosen
    if not fresh:
        given, *rest = rest
    if closing:
        *earlier, new_ref, out0, out1, out2, out3, grad_ref, peak_grad, places = rest
        out_refs = (out0, out1, out2, out3)
    else:
        new_ref, grad_ref, peak_grad, places = rest
    own_tiles = peak_ref.shape[0]
    row_tiles = grad_ref.shape[0] - 1
    slots = places.shape[0] - group_size

    def note(t, found):
        place = index[stratum, t]
        places[found] = place * slots + t
        mine = (place % peak_tiles) // own_tiles == part
        return found + jnp.where(mine, 1, 0)

    found = lax.fori_loop(0, counts[0, stratum], note, 0)
    for k in range(group_size):
        places[found + k] = -1
    peak_grad[...] = jnp.zeros_like(peak_grad)
    grad_ref[...] = jnp.zeros_like(grad_ref) if fresh else given[...]

    def slot_of(k):
        code = places[k]
        used = code >= 0
        code = jnp.maximum(code, 0)
        place = code // slots
        row, col = place // peak_tiles, place % own_tiles
        return code % slots, row, col, jnp.where(used, row, row_tiles), jnp.where(used, col, own_tiles)

    groups = (found + group_size - 1) // group_size
    walk(groups, slot_of, cell_ref, peak_ref, lambda t: values[0, t], peak_grad, grad_ref, scaling)
    for c in range(own_tiles):
        new_ref[c] = stepped(peak_ref[c], peak_grad[c], scaling)
    if closing:
        near = len(out_refs)
        spot = lax.axis_index("chrom") % near
        for parity, early in enumerate(earlier):

            @pl.when(lax.axis_index("cell") % 2 == parity)
            def _():
                for ahead in range(near):
                    for side in range(row_tiles // near):
                        row = (spot + ahead) % near + side * near
                        total = (early[row] + grad_ref[row]) * (gradient_scale * scaling)
                        out_refs[ahead][side] = total.astype(out_refs[ahead].dtype)


def token_kernel(piece_ref, token_ref):
    token_ref[...] = jnp.zeros_like(token_ref)


def place_kernel(part, piece_ref, *refs):
    out_ref, sem = refs[-2:]
    own_tiles = piece_ref.shape[0]
    copy = pltpu.make_async_copy(piece_ref, out_ref.at[pl.ds(part * own_tiles, own_tiles)], sem)
    copy.start()
    copy.wait()


def cost(flops, read):
    return pl.CostEstimate(flops=flops, bytes_accessed=read, transcendentals=0)


def per_device(cell_factors, peak_factors, tile_values, tile_index, tile_counts):
    cell_dev, rank_width = cell_factors.shape
    strata, slots, tile_size, _ = tile_values.shape
    block_rows = peak_factors.shape[0]
    row_tiles = cell_dev // tile_size
    peak_tiles = block_rows // tile_size
    own_tiles = peak_tiles // parts
    chroms = lax.axis_size("chrom")
    cells = lax.axis_size("cell")
    share_rows = cell_dev // chroms
    assert share_rows == tile_size
    near = chroms // 2
    scaling = 1.0 / math.sqrt(rank_width)
    flops = 6 * slots * tile_size * tile_size * rank_width
    cell_blocks = cell_factors.reshape(row_tiles, tile_size, rank_width)
    peak_block = peak_factors.reshape(peak_tiles, tile_size, rank_width)
    counts = tile_counts.T
    last = strata - 1

    def moved(piece, by):
        return lax.ppermute(piece, "cell", [(i, (i + by) % cells) for i in range(cells)])

    piece_out = jax.ShapeDtypeStruct((own_tiles, tile_size, rank_width), jnp.bfloat16)
    grad_out = jax.ShapeDtypeStruct((row_tiles + 1, tile_size, rank_width), jnp.float32)

    early_out = jax.ShapeDtypeStruct(cell_blocks.shape, jnp.float32)

    def first_call(parity, before):
        return pl.pallas_call(
            functools.partial(first_kernel, scaling, parity),
            grid=(1,),
            out_shape=(piece_out,) * parts + (early_out,),
            in_specs=[smem, smem, far, far, far] + [far] * len(before),
            out_specs=(vmem,) * (parts + 1),
            scratch_shapes=[
                pltpu.VMEM(cell_blocks.shape, jnp.bfloat16),
                pltpu.VMEM(peak_block.shape, jnp.bfloat16),
                pltpu.VMEM(tile_values.shape[1:], jnp.bfloat16),
                pltpu.VMEM(peak_block.shape, jnp.float32),
                pltpu.SemaphoreType.DMA((3,)),
            ],
            compiler_params=pltpu.CompilerParams(vmem_limit_bytes=60 * mebi),
            cost_estimate=cost(flops, 4 * mebi),
        )(counts, tile_index, cell_blocks, peak_block, tile_values, *before)

    *firsts, early_even = first_call(0, [])
    over = [moved(piece, -1) for piece in firsts]
    *seconds, early_odd = first_call(1, firsts[:1])
    swapped = [lax.ppermute(piece, "cell", [(i, i ^ 1) for i in range(cells)]) for piece in seconds]
    pieces = []
    for near_piece, far_piece in zip(swapped, over):
        token = pl.pallas_call(
            token_kernel,
            grid=(1,),
            out_shape=jax.ShapeDtypeStruct((8, lanes), jnp.int32),
            in_specs=[far],
            out_specs=vmem,
            compiler_params=pltpu.CompilerParams(vmem_limit_bytes=16 * mebi),
            cost_estimate=cost(0, 32 * mebi),
        )(far_piece)
        pieces.append((near_piece, far_piece, token))
    grad = None
    def part_call(stratum, part, piece, given, closing):
        own_values = pl.BlockSpec((1,) + tile_values.shape[1:], lambda i: (stratum, 0, 0, 0))
        paired = isinstance(piece, tuple)
        args = [counts, tile_index, cell_blocks, tile_values, *(piece if paired else (piece,))]
        if given is not None:
            args.append(given)
        if closing:
            args += [early_even, early_odd]
        in_specs = [smem, smem, vmem, own_values]
        in_specs += [vmem] * (len(args) - len(in_specs))
        scratch = [
            pltpu.VMEM((own_tiles + 1, tile_size, rank_width), jnp.float32),
            pltpu.SMEM((slots + group_size,), jnp.int32),
        ]
        if paired:
            scratch.append(pltpu.VMEM(piece_out.shape, jnp.bfloat16))
        others = (grad_out,)
        if closing:
            others = (jax.ShapeDtypeStruct((chroms // near, share_rows, rank_width), jnp.bfloat16),) * near
            scratch.insert(0, pltpu.VMEM(grad_out.shape, jnp.float32))
        return pl.pallas_call(
            functools.partial(part_kernel, scaling, stratum, part, peak_tiles, closing, paired, given is None),
            grid=(1,),
            out_shape=(piece_out,) + others,
            in_specs=in_specs,
            out_specs=(vmem,) * (1 + len(others)),
            scratch_shapes=scratch,
            compiler_params=pltpu.CompilerParams(vmem_limit_bytes=16 * mebi),
            cost_estimate=cost(flops // parts, 3 * mebi),
        )(*args)

    for stratum in range(1, strata):
        for part in range(parts):
            closing = stratum == last and part == parts - 1
            piece, *grads = part_call(stratum, part, pieces[part], grad, closing)
            grad = grads[0]
            pieces[part] = moved(piece, last if stratum == last else -1)

    def put(part, peak_out):
        args = [pieces[part]] + ([] if peak_out is None else [peak_out])
        return pl.pallas_call(
            functools.partial(place_kernel, part),
            grid=(1,),
            out_shape=jax.ShapeDtypeStruct(peak_block.shape, jnp.bfloat16),
            in_specs=[vmem, far][: len(args)],
            out_specs=far,
            scratch_shapes=[pltpu.SemaphoreType.DMA],
            input_output_aliases={} if peak_out is None else {1: 0},
            compiler_params=pltpu.CompilerParams(vmem_limit_bytes=16 * mebi),
            cost_estimate=cost(0, 8 * mebi),
        )(*args)

    around = [j // near * near for j in range(chroms)]
    shares = grads[:1] + [
        lax.ppermute(grads[d], "chrom", [(j, around[j] + (j + d) % near) for j in range(chroms)])
        for d in range(1, near)
    ]
    peak_out = None
    for part in range(parts - 1):
        peak_out = put(part, peak_out)
    peak_out, shares = lax.optimization_barrier((peak_out, shares))
    shares = sum(share.astype(jnp.float32) for share in shares)
    side = lax.axis_index("chrom") // near
    kept = lax.dynamic_index_in_dim(shares, side, 0, keepdims=False)
    sent = lax.dynamic_index_in_dim(shares, 1 - side, 0, keepdims=False).astype(jnp.bfloat16)
    got = lax.ppermute(sent, "chrom", [(j, (j + near) % chroms) for j in range(chroms)])
    summed = kept + got.astype(jnp.float32)
    summed, pieces[-1] = lax.optimization_barrier((summed, pieces[-1]))
    peak_out = put(parts - 1, peak_out)
    return (peak_out.reshape(block_rows, rank_width), summed)


def solution(mesh):
    in_specs = (
        P("cell", None),
        P(("cell", "chrom"), None),
        P("cell", "chrom", None, None),
        P("cell", "chrom"),
        P("cell", "chrom"),
    )
    out_specs = (P(("cell", "chrom"), None), P(("cell", "chrom"), None))
    return jax.shard_map(
        per_device, mesh=mesh, in_specs=in_specs, out_specs=out_specs, check_vma=False
    )
```

```python
import functools
import math

import jax
import jax.numpy as jnp
from jax import lax
from jax.experimental import pallas as pl
from jax.experimental.pallas import tpu as pltpu
from jax.sharding import PartitionSpec as P

learning_rate = 0.15
gradient_scale = 0.1
parts = 2
group_size = 8
lanes = 128
mebi = 1024 * 1024

smem = pl.BlockSpec(memory_space=pltpu.SMEM)
vmem = pl.BlockSpec(memory_space=pltpu.VMEM)
far = pl.BlockSpec(memory_space=pltpu.HBM)


def contract(left, right, dims):
    return lax.dot_general(left, right, ((dims[:1], dims[1:]), ((), ())), preferred_element_type=jnp.float32)


def split(value, size):
    assert size & (size - 1) == 0
    return value >> (size.bit_length() - 1), value & (size - 1)


def walk(groups, slot_of, cell_ref, peak_ref, values_at, peak_grad, grad_ref, scaling):
    def tiles(start, count):
        found = [slot_of(start + k) for k in range(count)]
        resids = []
        for t, row, col, _, _ in found:
            predicted = contract(cell_ref[row], peak_ref[col], (1, 1))
            resids.append((predicted * scaling - values_at(t).astype(jnp.float32)).astype(jnp.bfloat16))
        if peak_grad is not None:
            terms = [contract(r, cell_ref[f[1]], (0, 0)) for r, f in zip(resids, found)]
            for term, f in zip(terms, found):
                peak_grad[f[4]] += term
        if grad_ref is not None:
            terms = [contract(r, peak_ref[f[2]], (1, 0)) for r, f in zip(resids, found)]
            for term, f in zip(terms, found):
                grad_ref[f[3]] += term

    pairs = groups >> 1

    def pair(g, carry):
        tiles(g * 2 * group_size, 2 * group_size)
        return carry

    lax.fori_loop(0, pairs, pair, 0)

    @pl.when(groups > 2 * pairs)
    def _():
        tiles(pairs * 2 * group_size, group_size)


def stepped(peak, grad, scaling):
    return (peak.astype(jnp.float32) - learning_rate * (grad * scaling)).astype(jnp.bfloat16)


def first_kernel(scaling, counts, index, cell_in, peak_in, values_in, *refs):
    news, (cell_ref, peak_ref, values_ref, peak_grad, sems) = refs[:parts], refs[parts:]
    peak_tiles = peak_ref.shape[0]
    loads = [
        pltpu.make_async_copy(cell_in, cell_ref, sems.at[0]),
        pltpu.make_async_copy(peak_in, peak_ref, sems.at[1]),
        pltpu.make_async_copy(values_in.at[0], values_ref, sems.at[2]),
    ]
    for copy in loads:
        copy.start()
    peak_grad[...] = jnp.zeros_like(peak_grad)
    for copy in loads:
        copy.wait()

    def slot_of(t):
        place = index[0, t]
        row, col = split(place, peak_tiles)
        return t, row, col, row, col

    groups, _ = split(counts[0, 0], group_size)
    walk(groups, slot_of, cell_ref, peak_ref, lambda t: values_ref[t], peak_grad, None, scaling)
    own_tiles = peak_tiles // parts
    for c in range(peak_tiles):
        news[c // own_tiles][c % own_tiles] = stepped(peak_ref[c], peak_grad[c], scaling)


def cell_kernel(scaling, counts, index, cell_ref, peak_ref, values, grad_ref):
    peak_tiles = peak_ref.shape[0]
    grad_ref[...] = jnp.zeros_like(grad_ref)

    def slot_of(t):
        place = index[0, t]
        row, col = split(place, peak_tiles)
        return t, row, col, row, col

    groups, _ = split(counts[0, 0], group_size)
    walk(groups, slot_of, cell_ref, peak_ref, lambda t: values[0, t], None, grad_ref, scaling)


def part_kernel(scaling, stratum, part, peak_tiles, closing, fresh, *refs):
    counts, index, cell_ref, values, peak_ref, *rest = refs
    given = None
    if not fresh:
        given, *rest = rest
    if closing:
        new_ref, *out_refs, grad_ref, peak_grad, places = rest
    else:
        new_ref, grad_ref, peak_grad, places = rest
    own_tiles = peak_ref.shape[0]
    row_tiles = grad_ref.shape[0] - 1
    slots = places.shape[0] - group_size

    found = jnp.int32(0)
    live = counts[0, stratum]
    for t in range(slots):
        place = index[stratum, t]
        places[found] = place * slots + t
        owner, _ = split(split(place, peak_tiles)[1], own_tiles)
        found = found + jnp.where((owner == part) & (t < live), 1, 0)
    for k in range(group_size):
        places[found + k] = -1
    peak_grad[...] = jnp.zeros_like(peak_grad)
    grad_ref[...] = jnp.zeros_like(grad_ref) if fresh else given[...]

    def slot_of(k):
        code = places[k]
        used = code >= 0
        code = jnp.maximum(code, 0)
        place, t = split(code, slots)
        row, col = split(place, peak_tiles)
        col = split(col, own_tiles)[1]
        return t, row, col, jnp.where(used, row, row_tiles), jnp.where(used, col, own_tiles)

    groups, _ = split(found + group_size - 1, group_size)
    walk(groups, slot_of, cell_ref, peak_ref, lambda t: values[0, t], peak_grad, grad_ref, scaling)
    for c in range(own_tiles):
        new_ref[c] = stepped(peak_ref[c], peak_grad[c], scaling)
    if closing:
        near = len(out_refs)
        spot = lax.axis_index("chrom") % near
        for ahead in range(near):
            for side in range(row_tiles // near):
                row = (spot + ahead) % near + side * near
                total = grad_ref[row] * (gradient_scale * scaling)
                out_refs[ahead][side] = total.astype(out_refs[ahead].dtype)


def place_kernel(part, piece_ref, *refs):
    out_ref, sem = refs[-2:]
    own_tiles = piece_ref.shape[0]
    copy = pltpu.make_async_copy(piece_ref, out_ref.at[pl.ds(part * own_tiles, own_tiles)], sem)
    copy.start()
    copy.wait()


def cost(flops, read):
    return pl.CostEstimate(flops=flops, bytes_accessed=read, transcendentals=0)


def per_device(cell_factors, peak_factors, tile_values, tile_index, tile_counts):
    cell_dev, rank_width = cell_factors.shape
    strata, slots, tile_size, _ = tile_values.shape
    block_rows = peak_factors.shape[0]
    row_tiles = cell_dev // tile_size
    peak_tiles = block_rows // tile_size
    own_tiles = peak_tiles // parts
    chroms = lax.axis_size("chrom")
    cells = lax.axis_size("cell")
    share_rows = cell_dev // chroms
    assert share_rows == tile_size
    near = chroms // 2
    scaling = 1.0 / math.sqrt(rank_width)
    flops = 6 * slots * tile_size * tile_size * rank_width
    cell_blocks = cell_factors.reshape(row_tiles, tile_size, rank_width)
    peak_block = peak_factors.reshape(peak_tiles, tile_size, rank_width)
    counts = tile_counts.T
    last = strata - 1

    def moved(piece, by):
        return lax.ppermute(piece, "cell", [(i, (i + by) % cells) for i in range(cells)])

    piece_out = jax.ShapeDtypeStruct((own_tiles, tile_size, rank_width), jnp.bfloat16)
    grad_out = jax.ShapeDtypeStruct((row_tiles + 1, tile_size, rank_width), jnp.float32)

    pieces = pl.pallas_call(
        functools.partial(first_kernel, scaling),
        grid=(1,),
        out_shape=(piece_out,) * parts,
        in_specs=[smem, smem, far, far, far],
        out_specs=(vmem,) * parts,
        scratch_shapes=[
            pltpu.VMEM(cell_blocks.shape, jnp.bfloat16),
            pltpu.VMEM(peak_block.shape, jnp.bfloat16),
            pltpu.VMEM(tile_values.shape[1:], jnp.bfloat16),
            pltpu.VMEM(peak_block.shape, jnp.float32),
            pltpu.SemaphoreType.DMA((3,)),
        ],
        compiler_params=pltpu.CompilerParams(vmem_limit_bytes=60 * mebi),
        cost_estimate=cost(flops, 4 * mebi),
    )(counts, tile_index, cell_blocks, peak_block, tile_values)
    pieces = [moved(piece, -1) for piece in pieces]
    first_values = pl.BlockSpec((1,) + tile_values.shape[1:], lambda i: (0, 0, 0, 0))
    grad = pl.pallas_call(
        functools.partial(cell_kernel, scaling),
        grid=(1,),
        out_shape=grad_out,
        in_specs=[smem, smem, vmem, vmem, first_values],
        out_specs=vmem,
        compiler_params=pltpu.CompilerParams(vmem_limit_bytes=16 * mebi),
        cost_estimate=cost(flops, 4 * mebi),
    )(counts, tile_index, cell_blocks, peak_block, tile_values)

    def part_call(stratum, part, piece, given, closing):
        own_values = pl.BlockSpec((1,) + tile_values.shape[1:], lambda i: (stratum, 0, 0, 0))
        args = [counts, tile_index, cell_blocks, tile_values, piece]
        in_specs = [smem, smem, vmem, own_values, vmem]
        if given is not None:
            args.append(given)
        in_specs += [vmem] * (len(args) - len(in_specs))
        scratch = [
            pltpu.VMEM((own_tiles + 1, tile_size, rank_width), jnp.float32),
            pltpu.SMEM((slots + group_size,), jnp.int32),
        ]
        others = (grad_out,)
        if closing:
            others = (jax.ShapeDtypeStruct((chroms // near, share_rows, rank_width), jnp.bfloat16),) * near
            scratch.insert(0, pltpu.VMEM(grad_out.shape, jnp.float32))
        return pl.pallas_call(
            functools.partial(part_kernel, scaling, stratum, part, peak_tiles, closing, given is None),
            grid=(1,),
            out_shape=(piece_out,) + others,
            in_specs=in_specs,
            out_specs=(vmem,) * (1 + len(others)),
            scratch_shapes=scratch,
            compiler_params=pltpu.CompilerParams(vmem_limit_bytes=16 * mebi),
            cost_estimate=cost(flops // parts, 3 * mebi),
        )(*args)

    for stratum in range(1, strata):
        for part in range(parts):
            closing = stratum == last and part == parts - 1
            piece, *grads = part_call(stratum, part, pieces[part], grad, closing)
            grad = grads[0]
            pieces[part] = moved(piece, last if stratum == last else -1)

    def put(part, peak_out):
        args = [pieces[part]] + ([] if peak_out is None else [peak_out])
        return pl.pallas_call(
            functools.partial(place_kernel, part),
            grid=(1,),
            out_shape=jax.ShapeDtypeStruct(peak_block.shape, jnp.bfloat16),
            in_specs=[vmem, far][: len(args)],
            out_specs=far,
            scratch_shapes=[pltpu.SemaphoreType.DMA],
            input_output_aliases={} if peak_out is None else {1: 0},
            compiler_params=pltpu.CompilerParams(vmem_limit_bytes=16 * mebi),
            cost_estimate=cost(0, 8 * mebi),
        )(*args)

    around = [j // near * near for j in range(chroms)]
    shares = grads[:1] + [
        lax.ppermute(grads[d], "chrom", [(j, around[j] + (j + d) % near) for j in range(chroms)])
        for d in range(1, near)
    ]
    peak_out = None
    for part in range(parts - 1):
        peak_out = put(part, peak_out)
    peak_out, shares = lax.optimization_barrier((peak_out, shares))
    shares = sum(share.astype(jnp.float32) for share in shares)
    side = lax.axis_index("chrom") // near
    kept = lax.dynamic_index_in_dim(shares, side, 0, keepdims=False)
    sent = lax.dynamic_index_in_dim(shares, 1 - side, 0, keepdims=False).astype(jnp.bfloat16)
    got = lax.ppermute(sent, "chrom", [(j, (j + near) % chroms) for j in range(chroms)])
    summed = kept + got.astype(jnp.float32)
    summed, pieces[-1] = lax.optimization_barrier((summed, pieces[-1]))
    peak_out = put(parts - 1, peak_out)
    return (peak_out.reshape(block_rows, rank_width), summed)


def solution(mesh):
    in_specs = (
        P("cell", None),
        P(("cell", "chrom"), None),
        P("cell", "chrom", None, None),
        P("cell", "chrom"),
        P("cell", "chrom"),
    )
    out_specs = (P(("cell", "chrom"), None), P(("cell", "chrom"), None))
    return jax.shard_map(
        per_device, mesh=mesh, in_specs=in_specs, out_specs=out_specs, check_vma=False
    )
```

```python
import functools
import math

import jax
import jax.numpy as jnp
from jax import lax
from jax.experimental import pallas as pl
from jax.experimental.pallas import tpu as pltpu
from jax.sharding import PartitionSpec as P

learning_rate = 0.15
gradient_scale = 0.1
parts = 2
group_size = 8
lanes = 128
mebi = 1024 * 1024

smem = pl.BlockSpec(memory_space=pltpu.SMEM)
vmem = pl.BlockSpec(memory_space=pltpu.VMEM)
far = pl.BlockSpec(memory_space=pltpu.HBM)


def contract(left, right, dims):
    return lax.dot_general(left, right, ((dims[:1], dims[1:]), ((), ())), preferred_element_type=jnp.float32)


def split(value, size):
    assert size & (size - 1) == 0
    return value >> (size.bit_length() - 1), value & (size - 1)


def walk(groups, slot_of, cell_ref, peak_ref, values_at, peak_grad, grad_ref, scaling):
    def tiles(start, count):
        found = [slot_of(start + k) for k in range(count)]
        resids = []
        for t, row, col, _, _ in found:
            predicted = contract(cell_ref[row], peak_ref[col], (1, 1))
            resids.append((predicted * scaling - values_at(t).astype(jnp.float32)).astype(jnp.bfloat16))
        if peak_grad is not None:
            terms = [contract(r, cell_ref[f[1]], (0, 0)) for r, f in zip(resids, found)]
            for term, f in zip(terms, found):
                peak_grad[f[4]] += term
        if grad_ref is not None:
            terms = [contract(r, peak_ref[f[2]], (1, 0)) for r, f in zip(resids, found)]
            for term, f in zip(terms, found):
                grad_ref[f[3]] += term

    pairs = groups >> 1

    def pair(g, carry):
        tiles(g * 2 * group_size, 2 * group_size)
        return carry

    lax.fori_loop(0, pairs, pair, 0)

    @pl.when(groups > 2 * pairs)
    def _():
        tiles(pairs * 2 * group_size, group_size)


def stepped(peak, grad, scaling):
    return (peak.astype(jnp.float32) - learning_rate * (grad * scaling)).astype(jnp.bfloat16)


def first_kernel(scaling, parity, counts, index, cell_in, peak_in, values_in, *refs):
    news, (grad_ref, cell_ref, peak_ref, values_ref, peak_grad, sems) = refs[-6 - parts : -6], refs[-6:]
    peak_tiles = peak_ref.shape[0]

    @pl.when(lax.axis_index("cell") % 2 == parity)
    def _():
        loads = [
            pltpu.make_async_copy(cell_in, cell_ref, sems.at[0]),
            pltpu.make_async_copy(peak_in, peak_ref, sems.at[1]),
            pltpu.make_async_copy(values_in.at[0], values_ref, sems.at[2]),
        ]
        for copy in loads:
            copy.start()
        peak_grad[...] = jnp.zeros_like(peak_grad)
        grad_ref[...] = jnp.zeros_like(grad_ref)
        for copy in loads:
            copy.wait()

        def slot_of(t):
            place = index[0, t]
            row, col = split(place, peak_tiles)
            return t, row, col, row, col

        groups, _ = split(counts[0, 0], group_size)
        walk(groups, slot_of, cell_ref, peak_ref, lambda t: values_ref[t], peak_grad, grad_ref, scaling)
        own_tiles = peak_tiles // parts
        for c in range(peak_tiles):
            news[c // own_tiles][c % own_tiles] = stepped(peak_ref[c], peak_grad[c], scaling)


def part_kernel(scaling, stratum, part, peak_tiles, closing, paired, fresh, *refs):
    counts, index, cell_ref, values, peak_ref, *rest = refs
    if paired:
        far_ref, _, *rest, chosen = rest
        odd = lax.axis_index("cell") % 2

        @pl.when(odd == 0)
        def _():
            chosen[...] = peak_ref[...]

        @pl.when(odd == 1)
        def _():
            chosen[...] = far_ref[...]

        peak_ref = chosen
    if not fresh:
        given, *rest = rest
    if closing:
        *earlier, new_ref, out0, out1, out2, out3, grad_ref, peak_grad, places = rest
        out_refs = (out0, out1, out2, out3)
    else:
        new_ref, grad_ref, peak_grad, places = rest
    own_tiles = peak_ref.shape[0]
    row_tiles = grad_ref.shape[0] - 1
    slots = places.shape[0] - group_size

    found = jnp.int32(0)
    live = counts[0, stratum]
    for t in range(slots):
        place = index[stratum, t]
        places[found] = place * slots + t
        owner, _ = split(split(place, peak_tiles)[1], own_tiles)
        found = found + jnp.where((owner == part) & (t < live), 1, 0)
    for k in range(group_size):
        places[found + k] = -1
    peak_grad[...] = jnp.zeros_like(peak_grad)
    grad_ref[...] = jnp.zeros_like(grad_ref) if fresh else given[...]

    def slot_of(k):
        code = places[k]
        used = code >= 0
        code = jnp.maximum(code, 0)
        place, t = split(code, slots)
        row, col = split(place, peak_tiles)
        col = split(col, own_tiles)[1]
        return t, row, col, jnp.where(used, row, row_tiles), jnp.where(used, col, own_tiles)

    groups, _ = split(found + group_size - 1, group_size)
    walk(groups, slot_of, cell_ref, peak_ref, lambda t: values[0, t], peak_grad, grad_ref, scaling)
    for c in range(own_tiles):
        new_ref[c] = stepped(peak_ref[c], peak_grad[c], scaling)
    if closing:
        near = len(out_refs)
        spot = lax.axis_index("chrom") % near
        for parity, early in enumerate(earlier):

            @pl.when(lax.axis_index("cell") % 2 == parity)
            def _():
                for ahead in range(near):
                    for side in range(row_tiles // near):
                        row = (spot + ahead) % near + side * near
                        total = (early[row] + grad_ref[row]) * (gradient_scale * scaling)
                        out_refs[ahead][side] = total.astype(out_refs[ahead].dtype)


def token_kernel(piece_ref, token_ref):
    token_ref[...] = jnp.zeros_like(token_ref)


def place_kernel(part, piece_ref, *refs):
    out_ref, sem = refs[-2:]
    own_tiles = piece_ref.shape[0]
    copy = pltpu.make_async_copy(piece_ref, out_ref.at[pl.ds(part * own_tiles, own_tiles)], sem)
    copy.start()
    copy.wait()


def cost(flops, read):
    return pl.CostEstimate(flops=flops, bytes_accessed=read, transcendentals=0)


def per_device(cell_factors, peak_factors, tile_values, tile_index, tile_counts):
    cell_dev, rank_width = cell_factors.shape
    strata, slots, tile_size, _ = tile_values.shape
    block_rows = peak_factors.shape[0]
    row_tiles = cell_dev // tile_size
    peak_tiles = block_rows // tile_size
    own_tiles = peak_tiles // parts
    chroms = lax.axis_size("chrom")
    cells = lax.axis_size("cell")
    share_rows = cell_dev // chroms
    assert share_rows == tile_size
    near = chroms // 2
    scaling = 1.0 / math.sqrt(rank_width)
    flops = 6 * slots * tile_size * tile_size * rank_width
    cell_blocks = cell_factors.reshape(row_tiles, tile_size, rank_width)
    peak_block = peak_factors.reshape(peak_tiles, tile_size, rank_width)
    counts = tile_counts.T
    last = strata - 1

    def moved(piece, by):
        return lax.ppermute(piece, "cell", [(i, (i + by) % cells) for i in range(cells)])

    piece_out = jax.ShapeDtypeStruct((own_tiles, tile_size, rank_width), jnp.bfloat16)
    grad_out = jax.ShapeDtypeStruct((row_tiles + 1, tile_size, rank_width), jnp.float32)

    early_out = jax.ShapeDtypeStruct(cell_blocks.shape, jnp.float32)

    def first_call(parity, before):
        return pl.pallas_call(
            functools.partial(first_kernel, scaling, parity),
            grid=(1,),
            out_shape=(piece_out,) * parts + (early_out,),
            in_specs=[smem, smem, far, far, far] + [far] * len(before),
            out_specs=(vmem,) * (parts + 1),
            scratch_shapes=[
                pltpu.VMEM(cell_blocks.shape, jnp.bfloat16),
                pltpu.VMEM(peak_block.shape, jnp.bfloat16),
                pltpu.VMEM(tile_values.shape[1:], jnp.bfloat16),
                pltpu.VMEM(peak_block.shape, jnp.float32),
                pltpu.SemaphoreType.DMA((3,)),
            ],
            compiler_params=pltpu.CompilerParams(vmem_limit_bytes=60 * mebi),
            cost_estimate=cost(flops, 4 * mebi),
        )(counts, tile_index, cell_blocks, peak_block, tile_values, *before)

    *firsts, early_even = first_call(0, [])
    over = [moved(piece, -1) for piece in firsts]
    *seconds, early_odd = first_call(1, firsts[:1])
    swapped = [lax.ppermute(piece, "cell", [(i, i ^ 1) for i in range(cells)]) for piece in seconds]
    pieces = []
    for near_piece, far_piece in zip(swapped, over):
        token = pl.pallas_call(
            token_kernel,
            grid=(1,),
            out_shape=jax.ShapeDtypeStruct((8, lanes), jnp.int32),
            in_specs=[far],
            out_specs=vmem,
            compiler_params=pltpu.CompilerParams(vmem_limit_bytes=16 * mebi),
            cost_estimate=cost(0, 32 * mebi),
        )(far_piece)
        pieces.append((near_piece, far_piece, token))
    grad = None
    def part_call(stratum, part, piece, given, closing):
        own_values = pl.BlockSpec((1,) + tile_values.shape[1:], lambda i: (stratum, 0, 0, 0))
        paired = isinstance(piece, tuple)
        args = [counts, tile_index, cell_blocks, tile_values, *(piece if paired else (piece,))]
        if given is not None:
            args.append(given)
        if closing:
            args += [early_even, early_odd]
        in_specs = [smem, smem, vmem, own_values]
        in_specs += [vmem] * (len(args) - len(in_specs))
        scratch = [
            pltpu.VMEM((own_tiles + 1, tile_size, rank_width), jnp.float32),
            pltpu.SMEM((slots + group_size,), jnp.int32),
        ]
        if paired:
            scratch.append(pltpu.VMEM(piece_out.shape, jnp.bfloat16))
        others = (grad_out,)
        if closing:
            others = (jax.ShapeDtypeStruct((chroms // near, share_rows, rank_width), jnp.bfloat16),) * near
            scratch.insert(0, pltpu.VMEM(grad_out.shape, jnp.float32))
        return pl.pallas_call(
            functools.partial(part_kernel, scaling, stratum, part, peak_tiles, closing, paired, given is None),
            grid=(1,),
            out_shape=(piece_out,) + others,
            in_specs=in_specs,
            out_specs=(vmem,) * (1 + len(others)),
            scratch_shapes=scratch,
            compiler_params=pltpu.CompilerParams(vmem_limit_bytes=16 * mebi),
            cost_estimate=cost(flops // parts, 3 * mebi),
        )(*args)

    for stratum in range(1, strata):
        for part in range(parts):
            closing = stratum == last and part == parts - 1
            piece, *grads = part_call(stratum, part, pieces[part], grad, closing)
            grad = grads[0]
            pieces[part] = moved(piece, last if stratum == last else -1)

    def put(part, peak_out):
        args = [pieces[part]] + ([] if peak_out is None else [peak_out])
        return pl.pallas_call(
            functools.partial(place_kernel, part),
            grid=(1,),
            out_shape=jax.ShapeDtypeStruct(peak_block.shape, jnp.bfloat16),
            in_specs=[vmem, far][: len(args)],
            out_specs=far,
            scratch_shapes=[pltpu.SemaphoreType.DMA],
            input_output_aliases={} if peak_out is None else {1: 0},
            compiler_params=pltpu.CompilerParams(vmem_limit_bytes=16 * mebi),
            cost_estimate=cost(0, 8 * mebi),
        )(*args)

    around = [j // near * near for j in range(chroms)]
    shares = grads[:1] + [
        lax.ppermute(grads[d], "chrom", [(j, around[j] + (j + d) % near) for j in range(chroms)])
        for d in range(1, near)
    ]
    peak_out = None
    for part in range(parts - 1):
        peak_out = put(part, peak_out)
    peak_out, shares = lax.optimization_barrier((peak_out, shares))
    shares = sum(share.astype(jnp.float32) for share in shares)
    side = lax.axis_index("chrom") // near
    kept = lax.dynamic_index_in_dim(shares, side, 0, keepdims=False)
    sent = lax.dynamic_index_in_dim(shares, 1 - side, 0, keepdims=False).astype(jnp.bfloat16)
    got = lax.ppermute(sent, "chrom", [(j, (j + near) % chroms) for j in range(chroms)])
    summed = kept + got.astype(jnp.float32)
    summed, pieces[-1] = lax.optimization_barrier((summed, pieces[-1]))
    peak_out = put(parts - 1, peak_out)
    return (peak_out.reshape(block_rows, rank_width), summed)


def solution(mesh):
    in_specs = (
        P("cell", None),
        P(("cell", "chrom"), None),
        P("cell", "chrom", None, None),
        P("cell", "chrom"),
        P("cell", "chrom"),
    )
    out_specs = (P(("cell", "chrom"), None), P(("cell", "chrom"), None))
    return jax.shard_map(
        per_device, mesh=mesh, in_specs=in_specs, out_specs=out_specs, check_vma=False
    )
```
